128 devices in a mesh: row: 16 (over x, y_hi, core), col: 8 (over z, y_lo).
Axes of the slice: x: 4, y: 4 (y_hi: 2, y_lo: 2; y = y_hi * 2 + y_lo), z: 4, core: 2. Of those that a mesh axis runs over, the one named last changes fastest.
Arguments:
- precision: float32 [2, 8, 16, 16, 128, 128], P(None, 'col', None, 'row'), may hold values from -1 to 33, as said below
- features: bfloat16 [4096, 16, 16, 128], P('col', None, 'row'), may hold values from -0.75 to 0.75
- weights_q: int32 [4096], P('col'), may hold values from 1 to 64
Outputs:
- factored: float32 [2, 8, 16, 16, 128, 128], P(None, 'col', None, 'row')
The draws below stay inside these ranges and needn't reach their ends.
Inputs may be any that keep to these rules, and one draw needn't show every extreme that they name: `precision`: the top 2048 rows are symmetric; the leading 1024 x 1024 block is strictly diagonally dominant with a positive diagonal.
All inputs are finite; a program needn't handle non-finite values.
Results may differ from the reference program's by a relative error of at most 0.0023.
Values may be sent and summed in bfloat16 or wider, within the bound.
No kernel may reach another device: no remote copies, remote signals or barrier semaphores. Data moves between devices by JAX's collectives and lax.ppermute only.
A program may use at most 128 MiB of HBM per device.

```python
import jax
import jax.numpy as jnp
from jax import lax

M = 32768
B = 128
PW = 1024
WC = 2048
TR = 16
TCW = 2
IMPS = 4096
N_ROW = 16


def draw_precision(key, part):
    key = jax.random.fold_in(key, 11)
    first, second = jax.random.split(key, 2)
    base = jax.random.uniform(first, (M, WC), jnp.float32, -1.0, 1.0)
    top = base[:WC]
    top = 0.5 * (top + top.T)
    base = jnp.concatenate([top, base[WC:]], 0)
    row_ids = jnp.arange(M, dtype=jnp.int32)[:, None]
    col_ids = jnp.arange(WC, dtype=jnp.int32)[None, :]
    corner = (row_ids < PW) & (col_ids < PW)
    base = jnp.where(corner, base / 64.0, base)
    lift = 16.0 + 16.0 * jax.random.uniform(second, (WC,), jnp.float32)
    base = base + jnp.where(row_ids == col_ids, lift[None, :], 0.0)
    return base.reshape(TR, M // (TR * B), B, TCW, WC // (TCW * B), B).transpose(3, 4, 0, 1, 2, 5)


def with_ends(values, own_key, smallest, high):
    place = [jax.random.randint(jax.random.fold_in(own_key, axis), (), 0, length) for axis, length in enumerate(values.shape)]
    longest = values.shape.index(max(values.shape))
    next_to = place[:longest] + [(place[longest] + 1) % values.shape[longest]] + place[longest + 1:]
    return values.at[tuple(place)].set(smallest).at[tuple(next_to)].set(high)


def shard_levels(own_key, dims, pieces, smallest, largest):
    factor_of = 1.0
    for dim, shards_of in pieces:
        steps = jax.random.uniform(jax.random.fold_in(jax.random.fold_in(own_key, 6), dim), (shards_of,), jnp.float32, smallest / len(pieces), largest / len(pieces))
        factor_of = factor_of * jnp.repeat(jnp.exp(steps), dims[dim] // shards_of).reshape((-1,) + (1,) * (len(dims) - 1 - dim))
    return factor_of


def centred(own_key, shape, scale, limit, cuts=(), kind=jnp.bfloat16):
    values = scale * jax.random.normal(own_key, shape, jnp.float32)
    if cuts:
        values = values * shard_levels(own_key, shape, cuts, -0.22, 0.18)
    return jnp.clip(values, -limit, limit).astype(kind)


def setup_inputs(seed: int = 0) -> dict:
    key_list = jax.random.split(jax.random.key(seed), 4)
    return {
        "precision": draw_precision(jax.random.fold_in(key_list[3], 71), 0),
        "features": centred(key_list[1], (IMPS, TR, N_ROW, B), (IMPS // 64) ** -0.5, 0.75, ((0, 8), (2, 16))),
        "weights_q": with_ends(jax.random.randint(key_list[2], (IMPS,), 1, 65), jax.random.fold_in(key_list[2], 1), 1, 64).astype(jnp.int32),
    }


def reference(precision, features, weights_q):
    full = precision.transpose(2, 3, 4, 0, 1, 5).reshape(M, WC)
    flat = features.reshape(IMPS, M)
    scale = weights_q.astype(jnp.float32) / 64.0
    weighted = (scale[:, None] * flat[:, :WC]).astype(jnp.bfloat16)
    gram = lax.dot_general(flat.astype(jnp.float32), weighted.astype(jnp.float32), (((0,), (0,)), ((), ())), preferred_element_type=jnp.float32)
    summed = full + gram
    factor = jnp.linalg.cholesky(summed[:PW, :PW])
    inverse = jax.scipy.linalg.solve_triangular(factor, jnp.eye(PW, dtype=jnp.float32), lower=True)
    lower = lax.dot_general(summed[:, :PW].astype(jnp.float32), inverse.astype(jnp.float32), (((1,), (1,)), ((), ())), precision=lax.Precision.HIGHEST, preferred_element_type=jnp.float32)
    update = lax.dot_general(lower.astype(jnp.float32), lower[PW:WC].astype(jnp.float32), (((1,), (1,)), ((), ())), precision=lax.Precision.HIGHEST, preferred_element_type=jnp.float32)
    row_ids = jnp.arange(M, dtype=jnp.int32)[:, None]
    trailing = jnp.where(row_ids < PW, jnp.zeros_like(update), summed[:, PW:] - update)
    result = jnp.concatenate([lower, trailing], 1)
    return result.reshape(TR, M // (TR * B), B, TCW, WC // (TCW * B), B).transpose(3, 4, 0, 1, 2, 5)
```

```python
import jax
import jax.numpy as jnp
from jax import lax
from jax.sharding import PartitionSpec as P

PW = 1024
BF = jnp.bfloat16
F32 = jnp.float32


def split2(x):
    hi = x.astype(BF)
    return hi, (x - hi.astype(F32)).astype(BF)


def nt(a, b):
    return lax.dot_general(
        a,
        b,
        (((1,), (1,)), ((), ())),
        precision=lax.Precision.HIGH,
        preferred_element_type=F32,
    )


def factor_inverse(block):
    factor = jnp.linalg.cholesky(block)
    return jax.scipy.linalg.solve_triangular(
        factor, jnp.eye(block.shape[0], dtype=F32), lower=True
    )


def body(precision, features, weights_q):
    ncol = lax.axis_size("col")
    nrow = lax.axis_size("row")
    tcw = precision.shape[0]
    ta = precision.shape[2]
    side = precision.shape[4]
    count = features.shape[0]
    pt = PW // side
    tiles = precision.reshape(tcw, ta, side, side)
    xt = features.reshape(count, ta, side).transpose(1, 2, 0)
    hi, lo = split2(tiles[0, 0])
    pack = jnp.concatenate([xt[0], hi, lo], axis=1)
    got = lax.all_gather(lax.all_gather(pack, "col"), "row")
    window = got[..., :count]
    top = got[..., count : count + side].astype(F32) + got[..., count + side :].astype(F32)
    top = top.transpose(0, 2, 1, 3).reshape(nrow * side, PW)
    scale = lax.all_gather(weights_q, "col").astype(F32) / 64.0
    window = window.transpose(0, 2, 1, 3).reshape(nrow * side, ncol * count)
    weighted = (scale.reshape(1, -1) * window).astype(BF)
    rows = lax.all_to_all(xt.reshape(ncol, -1, count), "col", 0, 0, tiled=True)
    rows = rows.transpose(1, 0, 2).reshape(-1, ncol * count)
    prior = lax.all_to_all(tiles[0].reshape(ncol, -1, side), "col", 0, 0, tiled=True)
    prior = prior.transpose(1, 0, 2).reshape(-1, PW)
    gram = lax.dot_general(rows, weighted, (((1,), (1,)), ((), ())), preferred_element_type=F32)
    near = top + lax.dot_general(
        window, weighted[:PW], (((1,), (1,)), ((), ())), preferred_element_type=F32
    )
    inverse = factor_inverse(near[:PW])
    lower = nt(gram[:, :PW] + prior, inverse)
    below = nt(near[PW:], inverse)
    rest = gram[:, PW:] - nt(lower, below)
    back = jnp.stack([lower, rest]).reshape(tcw, -1, ncol, side).transpose(2, 0, 1, 3)
    back = lax.all_to_all(back, "col", 0, 0, tiled=True)
    back = back.transpose(1, 0, 2, 3).reshape(tcw, ta, side, side)
    row_tile = jnp.arange(ta, dtype=jnp.int32) * nrow + lax.axis_index("row")
    trailing = jnp.where(row_tile[:, None, None] < pt, 0.0, tiles[1] + back[1])
    result = jnp.stack([back[0], trailing])
    return result.reshape(tcw, 1, ta, 1, side, side)


def solution(mesh):
    in_specs = (P(None, "col", None, "row", None, None), P("col", None, "row", None), P("col"))
    out_specs = P(None, "col", None, "row", None, None)
    return jax.shard_map(body, mesh=mesh, in_specs=in_specs, out_specs=out_specs, check_vma=False)
```

```python
import functools

import jax
import jax.numpy as jnp
from jax import lax
from jax.experimental import pallas as pl
from jax.experimental.pallas import tpu as pltpu
from jax.sharding import PartitionSpec as P

PW = 1024
SIDE = 128
NC = 8
NQ = 4
BF = jnp.bfloat16
F32 = jnp.float32
NN = ((1,), (0,))
NT = ((1,), (1,))
TN = ((0,), (0,))
VMEM_LIMIT = 56 << 20


def dot6(a, b, dims=NN):
    return lax.dot_general(
        a, b, (dims, ((), ())), precision=lax.Precision.HIGHEST, preferred_element_type=F32
    )


def dot1(a, b, dims=NN):
    return lax.dot_general(a, b, (dims, ((), ())), preferred_element_type=F32)


def split2(x):
    hi = x.astype(BF)
    return hi, (x - hi.astype(F32)).astype(BF)


def flat(x, y, z, core):
    return ((x * 2 + y // 2) * 2 + core) * NC + z * 2 + y % 2


def shift_pairs(kind, by):
    out = []
    for x in range(4):
        for y in range(4):
            for z in range(4):
                for core in range(2):
                    nx, ny, nz, nc = x, y, z, core
                    if kind == "x":
                        nx = (x + by) % 4
                    elif kind == "core":
                        nc = 1 - core
                    elif (kind == "first") == (core == 0):
                        ny = (y + by) % 4
                    else:
                        nz = (z + by) % 4
                    out.append((flat(x, y, z, core), flat(nx, ny, nz, nc)))
    return out


def shift(x, kind, by=1):
    return lax.ppermute(x, ("row", "col"), shift_pairs(kind, by))


def ring(u, kind):
    half = u.shape[0] // 2
    prev = shift(u, kind, 1)
    nxt = shift(u, kind, -1)
    far0 = shift(prev[:half], kind, 1)
    far1 = shift(nxt[half:], kind, -1)
    return nxt, prev, far0, far1


def gather_plane(u):
    nxt, prev, far0, far1 = ring(u, "first")
    mine = jnp.stack([u, nxt, jnp.concatenate([far0, far1]), prev])
    nxt, prev, far0, far1 = ring(mine, "second")
    pieces = [mine, nxt, far0, far1, prev]
    return pieces + [shift(p, "core") for p in pieces]


PIECES = (((0, 1, 2, 3), 0), ((0, 1, 2, 3), 1), ((0, 1), 2), ((2, 3), 2), ((0, 1, 2, 3), 3))


def copies(pos_ref, piece_refs, buf, sems, width):
    out = []
    for n, ref in enumerate(piece_refs):
        firsts, second = PIECES[n % 5]
        core = pos_ref[2] if n < 5 else 1 - pos_ref[2]
        for i, first in enumerate(firsts):
            dy = jnp.where(core == 0, first, second)
            dz = jnp.where(core == 0, second, first)
            y = lax.rem(pos_ref[0] + dy, 4)
            z = lax.rem(pos_ref[1] + dz, 4)
            c = z * 2 + lax.rem(y, 2)
            q = lax.div(y, 2) * 2 + core
            out.append(
                pltpu.make_async_copy(
                    ref.at[i, :, :, pl.ds(0, width)], buf.at[c, q], sems.at[c]
                )
            )
    return out


def wait_chunk(piece_ref, buf, sems, c, width):
    for q in range(NQ):
        pltpu.make_async_copy(
            piece_ref.at[0, :, :, pl.ds(0, width)], buf.at[c, q], sems.at[c]
        ).wait()


def weigh(scale_ref, c, x):
    return (scale_ref[pl.ds(c, 1), :] * x.astype(F32)).astype(BF)


def top_kernel(pos_ref, scale_ref, *refs):
    pieces, (out_ref, buf, g_ref, sems) = refs[:10], refs[10:]
    width = buf.shape[-1]
    count = scale_ref.shape[-1]
    for copy in copies(pos_ref, pieces, buf, sems, width):
        copy.start()
    g_ref[...] = jnp.zeros_like(g_ref)

    def chunk(c, carry):
        wait_chunk(pieces[0], buf, sems, c, width)
        x = buf[c, :, :, :, :count].reshape(PW, count)
        g_ref[...] += dot1(x, weigh(scale_ref, c, x), NT)
        return carry

    lax.fori_loop(0, NC, chunk, 0)

    def tile(i, j):
        ri, rj = ((i % 4) * 2 + i // 4) * SIDE, ((j % 4) * 2 + j // 4) * SIDE
        return g_ref[ri : ri + SIDE, rj : rj + SIDE]

    for i in range(NC):
        for j in range(i + 1):
            prior = buf[j, i % 4, i // 4, :, count : count + 2 * SIDE].astype(F32)
            s = 0.5 * (tile(i, j) + tile(j, i).T) + (prior[:, :SIDE] + prior[:, SIDE:])
            out_ref[i * SIDE : (i + 1) * SIDE, j * SIDE : (j + 1) * SIDE] = s
            if j < i:
                out_ref[j * SIDE : (j + 1) * SIDE, i * SIDE : (i + 1) * SIDE] = s.T


def top_block(pos, scale, pieces):
    width = pieces[0].shape[-1]
    return pl.pallas_call(
        top_kernel,
        out_shape=jax.ShapeDtypeStruct((PW, PW), F32),
        in_specs=[
            pl.BlockSpec(memory_space=pltpu.SMEM),
            pl.BlockSpec(memory_space=pltpu.VMEM),
        ]
        + [pl.BlockSpec(memory_space=pl.ANY)] * 10,
        out_specs=pl.BlockSpec(memory_space=pltpu.VMEM),
        scratch_shapes=[
            pltpu.VMEM((NC, NQ, 2, SIDE, width), BF),
            pltpu.VMEM((PW, PW), F32),
            pltpu.SemaphoreType.DMA((NC,)),
        ],
        compiler_params=pltpu.CompilerParams(vmem_limit_bytes=VMEM_LIMIT),
    )(pos, scale, *pieces)


def rows_kernel(pos_ref, scale_ref, rows_ref, prior_ref, *refs):
    first, second = refs[:10], refs[10:20]
    near_ref, lead_ref, rest_ref, buf0, buf1, gn, gl, gr, sem0, sem1 = refs[20:]
    count = scale_ref.shape[-1]
    width = buf1.shape[-1]
    for copy in copies(pos_ref, first, buf0, sem0, count):
        copy.start()
    for copy in copies(pos_ref, second, buf1, sem1, width):
        copy.start()
    for ref in (gn, gl, gr):
        ref[...] = jnp.zeros_like(ref)

    def chunk(c, carry):
        wait_chunk(first[0], buf0, sem0, c, count)
        wait_chunk(second[0], buf1, sem1, c, width)
        w0 = weigh(scale_ref, c, buf0[c].reshape(PW, count))
        x1 = buf1[c, :, :, :, :count].reshape(PW, count)
        rows = rows_ref[c]
        gn[...] += dot1(x1, w0, NT)
        gl[...] += dot1(rows, w0, NT)
        gr[...] += dot1(rows, weigh(scale_ref, c, x1), NT)
        return carry

    lax.fori_loop(0, NC, chunk, 0)
    for j in range(NC):
        src = ((j % 4) * 2 + j // 4) * SIDE
        cols = slice(j * SIDE, (j + 1) * SIDE)
        lead_ref[:, cols] = gl[:, src : src + SIDE] + prior_ref[j]
        rest_ref[:, cols] = gr[:, src : src + SIDE]
        for i in range(NC):
            top = ((i % 4) * 2 + i // 4) * SIDE
            prior = buf1[j, i % 4, i // 4, :, count : count + 2 * SIDE].astype(F32)
            near_ref[i * SIDE : (i + 1) * SIDE, cols] = gn[
                top : top + SIDE, src : src + SIDE
            ] + (prior[:, :SIDE] + prior[:, SIDE:])


def own_rows(pos, scale, rows, prior, first, second):
    count = scale.shape[-1]
    width = first[0].shape[-1]
    own = rows.shape[1]
    vmem = pl.BlockSpec(memory_space=pltpu.VMEM)
    return pl.pallas_call(
        rows_kernel,
        out_shape=[
            jax.ShapeDtypeStruct((PW, PW), F32),
            jax.ShapeDtypeStruct((own, PW), F32),
            jax.ShapeDtypeStruct((own, PW), F32),
        ],
        in_specs=[pl.BlockSpec(memory_space=pltpu.SMEM), vmem, vmem, vmem]
        + [pl.BlockSpec(memory_space=pl.ANY)] * 20,
        out_specs=[vmem] * 3,
        scratch_shapes=[
            pltpu.VMEM((NC, NQ, 2, SIDE, count), BF),
            pltpu.VMEM((NC, NQ, 2, SIDE, width), BF),
            pltpu.VMEM((PW, PW), F32),
            pltpu.VMEM((own, PW), F32),
            pltpu.VMEM((own, PW), F32),
            pltpu.SemaphoreType.DMA((NC,)),
            pltpu.SemaphoreType.DMA((NC,)),
        ],
        compiler_params=pltpu.CompilerParams(vmem_limit_bytes=VMEM_LIMIT),
    )(pos, scale, rows, prior, *first, *second)


def factor(groups):
    m = list(groups)
    full = m[0].shape
    lane = lax.broadcasted_iota(jnp.int32, full, 1)
    sub = lax.broadcasted_iota(jnp.int32, full, 0)
    done = []
    for p in range(len(m)):
        base = 8 * p
        inside = (lane >= base) & (lane < base + 8)
        e = [jnp.broadcast_to(m[p][:, base + j : base + j + 1], full) for j in range(8)]
        s = {
            (l, j): jnp.broadcast_to(e[j][l : l + 1, :], full) for j in range(8) for l in range(j, 8)
        }
        own = jnp.where(inside, jnp.where(lane - base == sub, 1.0, 0.0), m[p])
        w = [jnp.broadcast_to(own[l : l + 1, :], full) for l in range(8)]
        t = {}
        v = [None] * 8
        for j in range(8):
            d = s[j, j]
            r = 1.0 / d
            v[j] = w[j] * lax.rsqrt(d)
            w[j] = w[j] * r
            for l in range(j + 1, 8):
                t[j, l] = s[l, j] * r
            for l in range(8):
                if l == j:
                    continue
                w[l] = w[l] - (s[l, j] if l > j else t[l, j]) * w[j]
                if l > j:
                    for k in range(j + 1, l + 1):
                        s[l, k] = s[l, k] - s[l, j] * t[j, k]
                else:
                    for k in range(j + 1, 8):
                        t[l, k] = t[l, k] - t[l, j] * t[j, k]
        for g in range(p + 1, len(m)):
            c = [jnp.broadcast_to(m[g][:, base + j : base + j + 1], full) * w[j] for j in range(8)]
            total = ((c[0] + c[1]) + (c[2] + c[3])) + ((c[4] + c[5]) + (c[6] + c[7]))
            m[g] = jnp.where(inside, 0.0, m[g]) - total
        rows = v[0]
        for j in range(1, 8):
            rows = jnp.where(sub == j, v[j], rows)
        done.append(jnp.where(lane <= sub + base, rows, 0.0))
    return done


def inverse_kernel(s_ref, inv_ref, a_ref, m_ref, z_ref):
    order = s_ref.shape[0]
    a_ref[...] = s_ref[...]
    eye = (
        lax.broadcasted_iota(jnp.int32, (SIDE, SIDE), 0)
        == lax.broadcasted_iota(jnp.int32, (SIDE, SIDE), 1)
    ).astype(F32)
    col = lax.broadcasted_iota(jnp.int32, (SIDE, order), 1)

    def step(k, carry):
        ko = pl.multiple_of(k * SIDE, SIDE)
        here = pl.ds(ko, SIDE)
        groups = [
            a_ref[pl.ds(pl.multiple_of(ko + 8 * g, 8), 8), here] for g in range(SIDE // 8)
        ]
        for g, rows in enumerate(factor(groups)):
            m_ref[8 * g : 8 * g + 8, :] = rows
        a_ref[here, here] = eye
        linv = m_ref[...]
        v = dot6(linv, a_ref[here, :])
        inv_ref[here, :] = jnp.where(col < ko + SIDE, v, 0.0)
        z_ref[...] = dot6(linv, v, TN)

        def below(i, carry):
            rows = pl.ds(pl.multiple_of(i * SIDE, SIDE), SIDE)
            left = a_ref[rows, here]
            a_ref[rows, here] = jnp.zeros((SIDE, SIDE), F32)
            a_ref[rows, :] = a_ref[rows, :] - dot6(left, z_ref[...])
            return carry

        lax.fori_loop(k + 1, order // SIDE, below, 0)
        return carry

    lax.fori_loop(0, order // SIDE, step, 0)


def factor_inverse(block):
    order = block.shape[0]
    return pl.pallas_call(
        inverse_kernel,
        out_shape=jax.ShapeDtypeStruct((order, order), F32),
        scratch_shapes=[
            pltpu.VMEM((order, order), F32),
            pltpu.VMEM((SIDE, SIDE), F32),
            pltpu.VMEM((SIDE, order), F32),
        ],
        compiler_params=pltpu.CompilerParams(vmem_limit_bytes=VMEM_LIMIT),
    )(block)


def dot3(a, b, dims):
    return dot1(a[0], b[0], dims) + (dot1(a[0], b[1], dims) + dot1(a[1], b[0], dims))


def solve_kernel(inv_ref, near_ref, lead_ref, rest_ref, out_ref, near_s, lead_s):
    step = 2 * SIDE
    for j in range(PW // step):
        k = (j + 1) * step
        cols = slice(j * step, k)
        inv = split2(inv_ref[cols, :k])
        for src, dst in ((near_ref, near_s), (lead_ref, lead_s)):
            hi, lo = split2(dot3(split2(src[:, :k]), inv, NT))
            dst[0, :, cols] = hi
            dst[1, :, cols] = lo
    for j in range(NC):
        cols = slice(j * SIDE, (j + 1) * SIDE)
        out_ref[j, 0] = lead_s[0, :, cols]
    for j in range(PW // step):
        cols = slice(j * step, (j + 1) * step)
        update = dot3((lead_s[0], lead_s[1]), (near_s[0, cols, :], near_s[1, cols, :]), NT)
        rest = (rest_ref[:, cols] - update).astype(BF)
        out_ref[2 * j, 1] = rest[:, :SIDE]
        out_ref[2 * j + 1, 1] = rest[:, SIDE:]


def solve_rows(inverse, near, lead, rest):
    own = lead.shape[0]
    return pl.pallas_call(
        solve_kernel,
        out_shape=jax.ShapeDtypeStruct((NC, 2, own, SIDE), BF),
        scratch_shapes=[pltpu.VMEM((2, PW, PW), BF), pltpu.VMEM((2, own, PW), BF)],
        compiler_params=pltpu.CompilerParams(vmem_limit_bytes=VMEM_LIMIT),
    )(inverse, near, lead, rest)


def body(precision, features, weights_q):
    tcw, ta = precision.shape[0], precision.shape[2]
    count = features.shape[0]
    row, col = lax.axis_index("row"), lax.axis_index("col")
    place = jnp.stack([(row // 2) % 2 * 2 + col % 2, col // 2, row % 2]).astype(jnp.int32)
    tiles = precision.reshape(tcw, ta, SIDE, SIDE)
    xt = features.reshape(count, ta, SIDE).transpose(1, 2, 0)
    hi = lax.reduce_precision(tiles[0, 0], 8, 7)
    lo = tiles[0, 0] - hi
    pack = jnp.concatenate([xt[0], hi.astype(BF), lo.astype(BF)], axis=1)
    weights = jnp.broadcast_to(weights_q.astype(BF), (NC, 16, count))
    scale = lax.all_to_all(weights, "col", 0, 0, tiled=True)[:, 0].astype(F32) / 64.0
    nxt, prev, far0, far1 = ring(pack, "x")
    line = jnp.stack([pack, nxt, jnp.concatenate([far0, far1]), prev])
    line = jnp.roll(line, row // 4, axis=0)
    first = gather_plane(line[:2])
    second = gather_plane(line[2:])
    rows = lax.all_to_all(xt.reshape(NC, -1, count), "col", 0, 0, tiled=True)
    prior = lax.all_to_all(tiles[0].reshape(NC, -1, SIDE), "col", 0, 0, tiled=True)
    inverse = factor_inverse(top_block(place, scale, first))
    near, lead, rest = own_rows(place, scale, rows, prior, first, second)
    back = solve_rows(inverse, near, lead, rest)
    back = lax.all_to_all(back, "col", 0, 0, tiled=True).astype(F32)
    back = back.transpose(1, 0, 2, 3).reshape(tcw, ta, SIDE, SIDE)
    row_tile = jnp.arange(ta, dtype=jnp.int32) * lax.axis_size("row") + row
    trailing = jnp.where(row_tile[:, None, None] < PW // SIDE, 0.0, tiles[1] + back[1])
    result = jnp.stack([back[0], trailing])
    return result.reshape(tcw, 1, ta, 1, SIDE, SIDE)


def solution(mesh):
    in_specs = (P(None, "col", None, "row", None, None), P("col", None, "row", None), P("col"))
    out_specs = P(None, "col", None, "row", None, None)
    return jax.shard_map(body, mesh=mesh, in_specs=in_specs, out_specs=out_specs, check_vma=False)
```

```python
import functools

import jax
import jax.numpy as jnp
from jax import lax
from jax.experimental import pallas as pl
from jax.experimental.pallas import tpu as pltpu
from jax.sharding import PartitionSpec as P

PW = 1024
SIDE = 128
NC = 8
NQ = 4
BF = jnp.bfloat16
F32 = jnp.float32
NN = ((1,), (0,))
NT = ((1,), (1,))
TN = ((0,), (0,))
VMEM_LIMIT = 56 << 20


def dot6(a, b, dims=NN):
    return lax.dot_general(
        a, b, (dims, ((), ())), precision=lax.Precision.HIGHEST, preferred_element_type=F32
    )


def dot1(a, b, dims=NN):
    return lax.dot_general(a, b, (dims, ((), ())), preferred_element_type=F32)


def split2(x):
    hi = x.astype(BF)
    return hi, (x - hi.astype(F32)).astype(BF)


def flat(x, y, z, core):
    return ((x * 2 + y // 2) * 2 + core) * NC + z * 2 + y % 2


def shift_pairs(kind, by):
    out = []
    for x in range(4):
        for y in range(4):
            for z in range(4):
                for core in range(2):
                    nx, ny, nz, nc = x, y, z, core
                    if kind == "x":
                        nx = (x + by) % 4
                    elif kind == "core":
                        nc = 1 - core
                    elif (kind == "first") == (core == 0):
                        ny = (y + by) % 4
                    else:
                        nz = (z + by) % 4
                    out.append((flat(x, y, z, core), flat(nx, ny, nz, nc)))
    return out


def shift(x, kind, by=1):
    return lax.ppermute(x, ("row", "col"), shift_pairs(kind, by))


def line_of(u, kind):
    return [u, shift(u, kind, -1), shift(u, kind, 2), shift(u, kind, 1)]


def far_halves(nxt, prev):
    half = nxt.shape[0] // 2
    return [shift(prev[:half], "second", 1), shift(nxt[half:], "second", -1)]


def to_other(pieces):
    return [shift(p, "core") for p in pieces]


def piece_at(first, second):
    if second == 2:
        return (3, first) if first < 2 else (4, first - 2)
    return ((0, 1, None, 2)[second], first)


def chip_of(pos_ref, i, j):
    core = pos_ref[2]
    y = lax.rem(pos_ref[0] + jnp.where(core == 0, i, j), 4)
    z = lax.rem(pos_ref[1] + jnp.where(core == 0, j, i), 4)
    return y, z


def copies(pos_ref, pieces, buf, sems, width):
    out = []
    for i0, j0 in ((0, 0), (0, 1), (1, 0), (1, 1)):
        for i, j in ((i0, j0), (i0 + 2, j0), (i0, j0 + 2), (i0 + 2, j0 + 2)):
            y, z = chip_of(pos_ref, i, j)
            c = z * 2 + lax.rem(y, 2)
            for other in range(2):
                core = 1 - pos_ref[2] if other else pos_ref[2]
                n, k = piece_at(j, i) if other else piece_at(i, j)
                out.append(
                    pltpu.make_async_copy(
                        pieces[5 * other + n].at[k, :, :, pl.ds(0, width)],
                        buf.at[c, lax.div(y, 2) * 2 + core],
                        sems.at[c],
                    )
                )
    return out


def chunk_at(pos_ref, t):
    i, j = lax.div(t, 4), lax.rem(lax.div(t, 2), 2)
    y, z = chip_of(pos_ref, i, j)
    return lax.rem(z + 2 * lax.rem(t, 2), 4) * 2 + lax.rem(y, 2)


def wait_chunk(piece_ref, buf, sems, c, width):
    for q in range(NQ):
        pltpu.make_async_copy(
            piece_ref.at[0, :, :, pl.ds(0, width)], buf.at[c, q], sems.at[c]
        ).wait()


def pack_kernel(features_ref, prior_ref, out_ref):
    count = features_ref.shape[0]
    for a in range(features_ref.shape[1]):
        out_ref[a, :, :count] = features_ref[:, a, :].T
        hi, lo = split2(prior_ref[a])
        out_ref[a, :, count : count + SIDE] = hi
        out_ref[a, :, count + SIDE :] = lo


def pack_rows(features, prior):
    count, ta, _ = features.shape
    return pl.pallas_call(
        pack_kernel,
        out_shape=jax.ShapeDtypeStruct((ta, SIDE, count + 2 * SIDE), BF),
        compiler_params=pltpu.CompilerParams(vmem_limit_bytes=VMEM_LIMIT),
    )(features, prior)


def weigh(scale_ref, c, x):
    return (scale_ref[pl.ds(c, 1), :] * x.astype(F32)).astype(BF)


def top_block(pos_ref, scale_ref, pieces, buf, wbuf, g_ref, a, sems):
    width = buf.shape[-1]
    count = scale_ref.shape[-1]
    for copy in copies(pos_ref, pieces, buf, sems, width):
        copy.start()
    g_ref[...] = jnp.zeros_like(g_ref)

    def weighted(t):
        c = chunk_at(pos_ref, t)
        x = buf[c, :, :, :, :count].reshape(PW, count)
        wbuf[lax.rem(t, 2)] = weigh(scale_ref, c, x)

    wait_chunk(pieces[0], buf, sems, chunk_at(pos_ref, 0), width)
    weighted(0)

    def chunk(t, carry):
        @pl.when(t + 1 < NC)
        def _():
            wait_chunk(pieces[0], buf, sems, chunk_at(pos_ref, t + 1), width)

        weighted(jnp.minimum(t + 1, NC - 1))
        x = buf[chunk_at(pos_ref, t), :, :, :, :count].reshape(PW, count)
        g_ref[...] += dot1(x, wbuf[lax.rem(t, 2)], NT)
        return carry

    lax.fori_loop(0, NC, chunk, 0)

    def tile(i, j):
        ri, rj = ((i % 4) * 2 + i // 4) * SIDE, ((j % 4) * 2 + j // 4) * SIDE
        return g_ref[ri : ri + SIDE, rj : rj + SIDE]

    for i in range(NC):
        for j in range(i, NC):
            prior = buf[j, i % 4, i // 4, :, count : count + 2 * SIDE].astype(F32)
            a[i * SIDE : (i + 1) * SIDE, j * SIDE : (j + 1) * SIDE] = 0.5 * (
                tile(i, j) + tile(j, i).T
            ) + (prior[:, :SIDE] + prior[:, SIDE:])


def factor(groups):
    m = list(groups)
    full = m[0].shape
    lane = lax.broadcasted_iota(jnp.int32, full, 1)
    sub = lax.broadcasted_iota(jnp.int32, full, 0)
    done = []
    for p in range(len(m)):
        base = 8 * p
        inside = (lane >= base) & (lane < base + 8)
        e = [jnp.broadcast_to(m[p][:, base + j : base + j + 1], full) for j in range(8)]
        s = {
            (l, j): jnp.broadcast_to(e[j][l : l + 1, :], full) for j in range(8) for l in range(j, 8)
        }
        own = jnp.where(inside, jnp.where(lane - base == sub, 1.0, 0.0), m[p])
        w = [jnp.broadcast_to(own[l : l + 1, :], full) for l in range(8)]
        t = {}
        v = [None] * 8
        for j in range(8):
            d = s[j, j]
            r = 1.0 / d
            v[j] = w[j] * lax.rsqrt(d)
            w[j] = w[j] * r
            for l in range(j + 1, 8):
                t[j, l] = s[l, j] * r
            for l in range(8):
                if l == j:
                    continue
                w[l] = w[l] - (s[l, j] if l > j else t[l, j]) * w[j]
                if l > j:
                    for k in range(j + 1, l + 1):
                        s[l, k] = s[l, k] - s[l, j] * t[j, k]
                else:
                    for k in range(j + 1, 8):
                        t[l, k] = t[l, k] - t[l, j] * t[j, k]
        for g in range(p + 1, len(m)):
            c = [jnp.broadcast_to(m[g][:, base + j : base + j + 1], full) * w[j] for j in range(8)]
            total = ((c[0] + c[1]) + (c[2] + c[3])) + ((c[4] + c[5]) + (c[6] + c[7]))
            m[g] = jnp.where(inside, 0.0, m[g]) - total
        rows = v[0]
        for j in range(1, 8):
            rows = jnp.where(sub == j, v[j], rows)
        done.append(jnp.where(lane <= sub + base, rows, 0.0))
    return done


def inverse_kernel(a_in, *refs, first, last):
    refs[-2][...] = a_in[...]
    block_steps(refs[:-2], *refs[-2:], first, last)


def top_kernel(pos_ref, scale_ref, *refs, last):
    pieces, outs, (buf, wbuf, g_ref, a, m_ref, sems) = refs[:10], refs[10:-6], refs[-6:]
    top_block(pos_ref, scale_ref, pieces, buf, wbuf, g_ref, a, sems)
    block_steps(outs, a, m_ref, 0, last)


def block_steps(outs, a, m_ref, first, last):
    inv_ref = outs[0]
    order = a.shape[1]
    nb = order // SIDE

    def rows(i):
        return slice((i - first) * SIDE, (i - first + 1) * SIDE)

    def cols(i, j):
        return slice(i * SIDE, j * SIDE)

    def below(k, i, v):
        vi = v[:, cols(i, i + 1)]
        left = dot6(vi, v[:, : (k + 1) * SIDE], TN)
        if k:
            a[rows(i), cols(0, k)] = a[rows(i), cols(0, k)] - left[:, : k * SIDE]
        a[rows(i), cols(k, k + 1)] = -left[:, k * SIDE :]
        start = i if i > k + 1 else i + 1
        if start < nb:
            a[rows(i), cols(start, nb)] = a[rows(i), cols(start, nb)] - dot6(
                vi, v[:, start * SIDE :], TN
            )

    later = []
    for k in range(first, last):
        here, own = rows(k), cols(k, k + 1)
        groups = [
            a[here.start + 8 * g : here.start + 8 * g + 8, own] for g in range(SIDE // 8)
        ]
        for g, group in enumerate(factor(groups)):
            m_ref[8 * g : 8 * g + 8, :] = group
        for k0, i, v in later:
            below(k0, i, v)
        later = []
        linv = m_ref[...]
        parts = [dot6(linv, a[here, cols(0, k)])] if k else []
        parts.append(linv)
        if k + 1 < nb:
            side = dot6(linv, a[here, cols(k + 1, k + 2)])
            diag = cols(k + 1, k + 2)
            a[rows(k + 1), diag] = a[rows(k + 1), diag] - dot6(side, side, TN)
            parts.append(side)
        if k + 2 < nb:
            parts.append(dot6(linv, a[here, cols(k + 2, nb)]))
        v = jnp.concatenate(parts, axis=1)
        inv_ref[here, : (k + 1) * SIDE] = v[:, : (k + 1) * SIDE]
        if k + 1 < nb:
            inv_ref[here, (k + 1) * SIDE :] = jnp.zeros((SIDE, order - (k + 1) * SIDE), F32)
        later = [(k, i, v) for i in range(k + 1, nb)]
    for k0, i, v in later:
        below(k0, i, v)
    if last < nb:
        outs[1][...] = a[(last - first) * SIDE :, :]


CUTS = (0, 3, 6, 8)


def step_shapes(first, last):
    shapes = [jax.ShapeDtypeStruct(((last - first) * SIDE, PW), F32)]
    if last < NC:
        shapes.append(jax.ShapeDtypeStruct((PW - last * SIDE, PW), F32))
    return shapes


def step_cost(us):
    return pl.CostEstimate(flops=us * 10**9, bytes_accessed=10**6, transcendentals=0)


def first_steps(pos, scale, pieces):
    width = pieces[0].shape[-1]
    return pl.pallas_call(
        functools.partial(top_kernel, last=CUTS[1]),
        out_shape=step_shapes(0, CUTS[1]),
        in_specs=[
            pl.BlockSpec(memory_space=pltpu.SMEM),
            pl.BlockSpec(memory_space=pltpu.VMEM),
        ]
        + [pl.BlockSpec(memory_space=pl.ANY)] * 10,
        out_specs=[pl.BlockSpec(memory_space=pltpu.VMEM)] * 2,
        scratch_shapes=[
            pltpu.VMEM((NC, NQ, 2, SIDE, width), BF),
            pltpu.VMEM((2, PW, scale.shape[1]), BF),
            pltpu.VMEM((PW, PW), F32),
            pltpu.VMEM((PW, PW), F32),
            pltpu.VMEM((SIDE, SIDE), F32),
            pltpu.SemaphoreType.DMA((NC,)),
        ],
        compiler_params=pltpu.CompilerParams(vmem_limit_bytes=VMEM_LIMIT),
        cost_estimate=step_cost(40),
    )(pos, scale, *pieces)


def more_steps(block, first, last):
    return pl.pallas_call(
        functools.partial(inverse_kernel, first=first, last=last),
        out_shape=step_shapes(first, last),
        scratch_shapes=[pltpu.VMEM(block.shape, F32), pltpu.VMEM((SIDE, SIDE), F32)],
        compiler_params=pltpu.CompilerParams(vmem_limit_bytes=VMEM_LIMIT),
        cost_estimate=step_cost(1),
    )(block)


def dot3(a, b, dims):
    return dot1(a[0], b[0], dims) + (dot1(a[0], b[1], dims) + dot1(a[1], b[0], dims))


def rows_kernel(pos_ref, scale_ref, rows_ref, *refs):
    inv_refs, first, second, refs = refs[:3], refs[3:13], refs[13:23], refs[23:]
    out_ref, buf0, buf1, w0, w1, gn, gl, gr, near, lead, near_s, lead_s, sem0, sem1 = refs
    count = scale_ref.shape[-1]
    width = buf1.shape[-1]
    own = rows_ref.shape[1]
    for one, two in zip(
        copies(pos_ref, first, buf0, sem0, count), copies(pos_ref, second, buf1, sem1, width)
    ):
        one.start()
        two.start()
    for ref in (gn, gl, gr):
        ref[...] = jnp.zeros_like(ref)

    def arrive(t):
        c = chunk_at(pos_ref, t)
        wait_chunk(first[0], buf0, sem0, c, count)
        wait_chunk(second[0], buf1, sem1, c, width)

    def weighted(t):
        c = chunk_at(pos_ref, t)
        w0[lax.rem(t, 2)] = weigh(scale_ref, c, buf0[c].reshape(PW, count))
        w1[lax.rem(t, 2)] = weigh(scale_ref, c, buf1[c, :, :, :, :count].reshape(PW, count))

    arrive(0)
    weighted(0)

    def chunk(t, carry):
        @pl.when(t + 1 < NC)
        def _():
            arrive(t + 1)

        weighted(jnp.minimum(t + 1, NC - 1))
        c = chunk_at(pos_ref, t)
        x1 = buf1[c, :, :, :, :count].reshape(PW, count)
        rows = rows_ref[c, :, :count]
        gn[...] += dot1(x1, w0[lax.rem(t, 2)], NT)
        gl[...] += dot1(rows, w0[lax.rem(t, 2)], NT)
        gr[...] += dot1(rows, w1[lax.rem(t, 2)], NT)
        return carry

    lax.fori_loop(0, NC, chunk, 0)

    def source(j):
        start = ((j % 4) * 2 + j // 4) * SIDE
        return slice(start, start + SIDE)

    for j in range(NC):
        cols = slice(j * SIDE, (j + 1) * SIDE)
        prior = rows_ref[j, :, count:].astype(F32)
        lead[:, cols] = gl[:, source(j)] + (prior[:, :SIDE] + prior[:, SIDE:])
        for i in range(NC):
            prior = buf1[j, i % 4, i // 4, :, count : count + 2 * SIDE].astype(F32)
            near[i * SIDE : (i + 1) * SIDE, cols] = gn[source(i), source(j)] + (
                prior[:, :SIDE] + prior[:, SIDE:]
            )

    def inverse_block(j):
        part = [j >= cut for cut in CUTS].index(False) - 1
        row = (j - CUTS[part]) * SIDE
        return inv_refs[part][row : row + SIDE, :]

    step = 2 * SIDE
    for j in range(PW // step):
        k = (j + 1) * step
        cols = slice(j * step, k)
        inv = split2(
            jnp.concatenate([inverse_block(2 * j)[:, :k], inverse_block(2 * j + 1)[:, :k]])
        )
        for src, dst in ((near, near_s), (lead, lead_s)):
            hi, lo = split2(dot3(split2(src[:, :k]), inv, NT))
            dst[0, :, cols] = hi
            dst[1, :, cols] = lo
    for j in range(NC):
        cols = slice(j * SIDE, (j + 1) * SIDE)
        out_ref[j, 0] = lead_s[0, :, cols]
        update = dot3((lead_s[0], lead_s[1]), (near_s[0, cols, :], near_s[1, cols, :]), NT)
        out_ref[j, 1] = (gr[:, source(j)] - update).astype(BF)


def own_rows(pos, scale, rows, inverse, first, second):
    count = scale.shape[-1]
    width = first[0].shape[-1]
    own = rows.shape[1]
    vmem = pl.BlockSpec(memory_space=pltpu.VMEM)
    return pl.pallas_call(
        rows_kernel,
        out_shape=jax.ShapeDtypeStruct((NC, 2, own, SIDE), BF),
        in_specs=[pl.BlockSpec(memory_space=pltpu.SMEM)]
        + [vmem] * 5
        + [pl.BlockSpec(memory_space=pl.ANY)] * 20,
        out_specs=vmem,
        scratch_shapes=[
            pltpu.VMEM((NC, NQ, 2, SIDE, count), BF),
            pltpu.VMEM((NC, NQ, 2, SIDE, width), BF),
            pltpu.VMEM((2, PW, count), BF),
            pltpu.VMEM((2, PW, count), BF),
            pltpu.VMEM((PW, PW), F32),
            pltpu.VMEM((own, PW), F32),
            pltpu.VMEM((own, PW), F32),
            pltpu.VMEM((PW, PW), F32),
            pltpu.VMEM((own, PW), F32),
            pltpu.VMEM((2, PW, PW), BF),
            pltpu.VMEM((2, own, PW), BF),
            pltpu.SemaphoreType.DMA((NC,)),
            pltpu.SemaphoreType.DMA((NC,)),
        ],
        compiler_params=pltpu.CompilerParams(vmem_limit_bytes=VMEM_LIMIT),
    )(pos, scale, rows, *inverse, *first, *second)


def body(precision, features, weights_q):
    tcw, ta = precision.shape[0], precision.shape[2]
    count = features.shape[0]
    row, col = lax.axis_index("row"), lax.axis_index("col")
    place = jnp.stack([(row // 2) % 2 * 2 + col % 2, col // 2, row % 2]).astype(jnp.int32)
    tiles = precision.reshape(tcw, ta, SIDE, SIDE)
    hi = lax.reduce_precision(tiles[0, 0], 8, 7)
    lo = tiles[0, 0] - hi
    pack = jnp.concatenate([features[:, 0, 0].T, hi.astype(BF), lo.astype(BF)], axis=1)
    weights = jnp.broadcast_to(weights_q.astype(BF), (NC, 16, count))
    pack, weights = lax.optimization_barrier((pack, weights))
    line = line_of(pack, "x")
    scale = lax.all_to_all(weights, "col", 0, 0, tiled=True)[:, 0].astype(F32) / 64.0
    line = [lax.select_n((x - row // 4) % 4, *line) for x in range(4)]
    packed = pack_rows(features.reshape(count, ta, SIDE), tiles[0])
    near_x, far_x = jnp.stack(line[:2]), jnp.stack(line[2:])
    line = line_of(near_x, "first")
    mine, scale, packed = lax.optimization_barrier((jnp.stack(line), scale, packed))
    nxt, prev = shift(mine, "second", -1), shift(mine, "second", 1)
    first = [mine, nxt, prev] + far_halves(nxt, prev)
    far_x, packed = lax.optimization_barrier((far_x, packed, first[3], first[4]))[:2]
    first += to_other(first)
    rows = lax.all_to_all(packed.reshape(NC, -1, packed.shape[2]), "col", 0, 0, tiled=True)
    far_line = line_of(far_x, "first")
    inv0, block = first_steps(place, scale, first)
    far_line, block, rows = lax.optimization_barrier((far_line, block, rows))
    mine = jnp.stack(far_line)
    nxt, prev = shift(mine, "second", -1), shift(mine, "second", 1)
    inv1, block = more_steps(block, CUTS[1], CUTS[2])
    mine, nxt, prev, block = lax.optimization_barrier((mine, nxt, prev, block))
    far = far_halves(nxt, prev)
    others = to_other([mine, nxt, prev])
    inv2 = more_steps(block, CUTS[2], CUTS[3])[0]
    far, inv2 = lax.optimization_barrier((far, inv2))
    second = [mine, nxt, prev] + far + others + to_other(far)
    back = own_rows(place, scale, rows, [inv0, inv1, inv2], first, second)
    back = lax.all_to_all(back, "col", 0, 0, tiled=True).astype(F32)
    back = back.transpose(1, 0, 2, 3).reshape(tcw, ta, SIDE, SIDE)
    row_tile = jnp.arange(ta, dtype=jnp.int32) * lax.axis_size("row") + row
    trailing = jnp.where(row_tile[:, None, None] < PW // SIDE, 0.0, tiles[1] + back[1])
    result = jnp.stack([back[0], trailing])
    return result.reshape(tcw, 1, ta, 1, SIDE, SIDE)


def solution(mesh):
    in_specs = (P(None, "col", None, "row", None, None), P("col", None, "row", None), P("col"))
    out_specs = P(None, "col", None, "row", None, None)
    return jax.shard_map(body, mesh=mesh, in_specs=in_specs, out_specs=out_specs, check_vma=False)
```

```python
import functools

import jax
import jax.numpy as jnp
from jax import lax
from jax.experimental import pallas as pl
from jax.experimental.pallas import tpu as pltpu
from jax.sharding import PartitionSpec as P

PW = 1024
SIDE = 128
NC = 8
NQ = 4
BF = jnp.bfloat16
F32 = jnp.float32
NN = ((1,), (0,))
NT = ((1,), (1,))
TN = ((0,), (0,))
VMEM_LIMIT = 56 << 20


def dot6(a, b, dims=NN):
    return lax.dot_general(
        a, b, (dims, ((), ())), precision=lax.Precision.HIGHEST, preferred_element_type=F32
    )


def dot1(a, b, dims=NN):
    return lax.dot_general(a, b, (dims, ((), ())), preferred_element_type=F32)


def split2(x):
    hi = x.astype(BF)
    return hi, (x - hi.astype(F32)).astype(BF)


def flat(x, y, z, core):
    return ((x * 2 + y // 2) * 2 + core) * NC + z * 2 + y % 2


def shift_pairs(kind, by):
    out = []
    for x in range(4):
        for y in range(4):
            for z in range(4):
                for core in range(2):
                    nx, ny, nz, nc = x, y, z, core
                    if kind == "x":
                        nx = (x + by) % 4
                    elif kind == "core":
                        nc = 1 - core
                    elif (kind == "first") == (core == 0):
                        ny = (y + by) % 4
                    else:
                        nz = (z + by) % 4
                    out.append((flat(x, y, z, core), flat(nx, ny, nz, nc)))
    return out


def shift(x, kind, by=1):
    return lax.ppermute(x, ("row", "col"), shift_pairs(kind, by))


def line_of(u, kind):
    return [u, shift(u, kind, -1), shift(u, kind, 2), shift(u, kind, 1)]


def far_halves(nxt, prev):
    half = nxt.shape[0] // 2
    return [shift(prev[:half], "second", 1), shift(nxt[half:], "second", -1)]


def to_other(pieces):
    return [shift(p, "core") for p in pieces]


def piece_at(first, second):
    if second == 2:
        return (3, first) if first < 2 else (4, first - 2)
    return ((0, 1, None, 2)[second], first)


def chip_of(pos_ref, i, j):
    core = pos_ref[2]
    y = lax.rem(pos_ref[0] + jnp.where(core == 0, i, j), 4)
    z = lax.rem(pos_ref[1] + jnp.where(core == 0, j, i), 4)
    return y, z


def copies(pos_ref, pieces, buf, sems, width):
    out = []
    for i0, j0 in ((0, 0), (0, 1), (1, 0), (1, 1)):
        for i, j in ((i0, j0), (i0 + 2, j0), (i0, j0 + 2), (i0 + 2, j0 + 2)):
            y, z = chip_of(pos_ref, i, j)
            c = z * 2 + lax.rem(y, 2)
            for other in range(2):
                core = 1 - pos_ref[2] if other else pos_ref[2]
                n, k = piece_at(j, i) if other else piece_at(i, j)
                out.append(
                    pltpu.make_async_copy(
                        pieces[5 * other + n].at[k, :, :, pl.ds(0, width)],
                        buf.at[c, lax.div(y, 2) * 2 + core],
                        sems.at[c],
                    )
                )
    return out


def chunk_at(pos_ref, t):
    i, j = lax.div(t, 4), lax.rem(lax.div(t, 2), 2)
    y, z = chip_of(pos_ref, i, j)
    return lax.rem(z + 2 * lax.rem(t, 2), 4) * 2 + lax.rem(y, 2)


def wait_chunk(piece_ref, buf, sems, c, width):
    for q in range(NQ):
        pltpu.make_async_copy(
            piece_ref.at[0, :, :, pl.ds(0, width)], buf.at[c, q], sems.at[c]
        ).wait()


def pack_kernel(features_ref, prior_ref, out_ref):
    count = features_ref.shape[0]
    for a in range(features_ref.shape[1]):
        out_ref[a, :, :count] = features_ref[:, a, :].T
        hi, lo = split2(prior_ref[a])
        out_ref[a, :, count : count + SIDE] = hi
        out_ref[a, :, count + SIDE :] = lo


def pack_rows(features, prior):
    count, ta, _ = features.shape
    return pl.pallas_call(
        pack_kernel,
        out_shape=jax.ShapeDtypeStruct((ta, SIDE, count + 2 * SIDE), BF),
        compiler_params=pltpu.CompilerParams(vmem_limit_bytes=VMEM_LIMIT),
    )(features, prior)


def weigh(scale_ref, c, x):
    return (scale_ref[pl.ds(c, 1), :] * x.astype(F32)).astype(BF)


def top_block(pos_ref, scale_ref, pieces, buf, wbuf, g_ref, a, sems):
    width = buf.shape[-1]
    count = scale_ref.shape[-1]
    moves = copies(pos_ref, pieces, buf, sems, width)

    def fetch(t):
        for copy in moves[4 * t : 4 * t + 8]:
            copy.start()

    fetch(0)
    g_ref[...] = jnp.zeros_like(g_ref)

    def weighted(t):
        c = chunk_at(pos_ref, t)
        x = buf[c, :, :, :, :count].reshape(PW, count)
        wbuf[lax.rem(t, 2)] = weigh(scale_ref, c, x)

    wait_chunk(pieces[0], buf, sems, chunk_at(pos_ref, 0), width)
    fetch(2)
    weighted(0)

    def chunk(t, carry):
        for ahead in range(4, NC, 2):

            @pl.when(t == ahead - 3)
            def _():
                fetch(ahead)

        @pl.when(t + 1 < NC)
        def _():
            wait_chunk(pieces[0], buf, sems, chunk_at(pos_ref, t + 1), width)

        weighted(jnp.minimum(t + 1, NC - 1))
        x = buf[chunk_at(pos_ref, t), :, :, :, :count].reshape(PW, count)
        g_ref[...] += dot1(x, wbuf[lax.rem(t, 2)], NT)
        return carry

    lax.fori_loop(0, NC, chunk, 0)

    def tile(i, j):
        ri, rj = ((i % 4) * 2 + i // 4) * SIDE, ((j % 4) * 2 + j // 4) * SIDE
        return g_ref[ri : ri + SIDE, rj : rj + SIDE]

    for i in range(NC):
        for j in range(i, NC):
            prior = buf[j, i % 4, i // 4, :, count : count + 2 * SIDE].astype(F32)
            a[i * SIDE : (i + 1) * SIDE, j * SIDE : (j + 1) * SIDE] = 0.5 * (
                tile(i, j) + tile(j, i).T
            ) + (prior[:, :SIDE] + prior[:, SIDE:])


def factor(groups, spread):
    m = list(groups)
    full = m[0].shape
    lane = lax.broadcasted_iota(jnp.int32, full, 1)
    sub = lax.broadcasted_iota(jnp.int32, full, 0)
    done = []
    for p in range(len(m)):
        base = 8 * p
        inside = (lane >= base) & (lane < base + 8)
        e = [jnp.broadcast_to(m[p][:, base + j : base + j + 1], full) for j in range(8)]
        for j in range(8):
            spread[p, 8 * j : 8 * j + 8, :] = e[j]
        s = {
            (l, j): jnp.broadcast_to(spread[p, 8 * j + l : 8 * j + l + 1, :], full)
            for j in range(8)
            for l in range(j, 8)
        }
        own = jnp.where(inside, jnp.where(lane - base == sub, 1.0, 0.0), m[p])
        w = [jnp.broadcast_to(own[l : l + 1, :], full) for l in range(8)]
        t = {}
        v = [None] * 8
        for j in range(8):
            d = s[j, j]
            r = 1.0 / d
            v[j] = w[j] * lax.rsqrt(d)
            w[j] = w[j] * r
            for l in range(j + 1, 8):
                t[j, l] = s[l, j] * r
            for l in range(8):
                if l == j:
                    continue
                w[l] = w[l] - (s[l, j] if l > j else t[l, j]) * w[j]
                if l > j:
                    for k in range(j + 1, l + 1):
                        s[l, k] = s[l, k] - s[l, j] * t[j, k]
                else:
                    for k in range(j + 1, 8):
                        t[l, k] = t[l, k] - t[l, j] * t[j, k]
        for g in range(p + 1, len(m)):
            c = [jnp.broadcast_to(m[g][:, base + j : base + j + 1], full) * w[j] for j in range(8)]
            total = ((c[0] + c[1]) + (c[2] + c[3])) + ((c[4] + c[5]) + (c[6] + c[7]))
            m[g] = jnp.where(inside, 0.0, m[g]) - total
        rows = v[0]
        for j in range(1, 8):
            rows = jnp.where(sub == j, v[j], rows)
        done.append(jnp.where(lane <= sub + base, rows, 0.0))
    return done


def inverse_kernel(a_in, *refs, first, last):
    refs[-3][...] = a_in[...]
    block_steps(refs[:-3], *refs[-3:], first, last)


def top_kernel(pos_ref, scale_ref, *refs, last):
    pieces, outs, (buf, wbuf, g_ref, a, m_ref, spread, sems) = refs[:10], refs[10:-7], refs[-7:]
    top_block(pos_ref, scale_ref, pieces, buf, wbuf, g_ref, a, sems)
    block_steps(outs, a, m_ref, spread, 0, last)


def block_steps(outs, a, m_ref, spread, first, last):
    inv_ref = outs[0]
    order = a.shape[1]
    nb = order // SIDE

    def rows(i):
        return slice((i - first) * SIDE, (i - first + 1) * SIDE)

    def cols(i, j):
        return slice(i * SIDE, j * SIDE)

    def below(k, i, v):
        vi = v[:, cols(i, i + 1)]
        left = dot6(vi, v[:, : (k + 1) * SIDE], TN)
        if k:
            a[rows(i), cols(0, k)] = a[rows(i), cols(0, k)] - left[:, : k * SIDE]
        a[rows(i), cols(k, k + 1)] = -left[:, k * SIDE :]
        start = i if i > k + 1 else i + 1
        if start < nb:
            a[rows(i), cols(start, nb)] = a[rows(i), cols(start, nb)] - dot6(
                vi, v[:, start * SIDE :], TN
            )

    later = []
    for k in range(first, last):
        here, own = rows(k), cols(k, k + 1)
        groups = [
            a[here.start + 8 * g : here.start + 8 * g + 8, own] for g in range(SIDE // 8)
        ]
        for g, group in enumerate(factor(groups, spread)):
            m_ref[8 * g : 8 * g + 8, :] = group
        for k0, i, v in later:
            below(k0, i, v)
        later = []
        linv = m_ref[...]
        parts = [dot6(linv, a[here, cols(0, k)])] if k else []
        parts.append(linv)
        if k + 1 < nb:
            side = dot6(linv, a[here, cols(k + 1, k + 2)])
            diag = cols(k + 1, k + 2)
            a[rows(k + 1), diag] = a[rows(k + 1), diag] - dot6(side, side, TN)
            parts.append(side)
        if k + 2 < nb:
            parts.append(dot6(linv, a[here, cols(k + 2, nb)]))
        v = jnp.concatenate(parts, axis=1)
        inv_ref[here, : (k + 1) * SIDE] = v[:, : (k + 1) * SIDE]
        if k + 1 < nb:
            inv_ref[here, (k + 1) * SIDE :] = jnp.zeros((SIDE, order - (k + 1) * SIDE), F32)
        later = [(k, i, v) for i in range(k + 1, nb)]
    for k0, i, v in later:
        below(k0, i, v)
    if last < nb:
        outs[1][...] = a[(last - first) * SIDE :, :]


CUTS = (0, 3, 6, 8)


def step_shapes(first, last):
    shapes = [jax.ShapeDtypeStruct(((last - first) * SIDE, PW), F32)]
    if last < NC:
        shapes.append(jax.ShapeDtypeStruct((PW - last * SIDE, PW), F32))
    return shapes


def step_cost(us):
    return pl.CostEstimate(flops=us * 10**9, bytes_accessed=10**6, transcendentals=0)


def first_steps(pos, scale, pieces):
    width = pieces[0].shape[-1]
    return pl.pallas_call(
        functools.partial(top_kernel, last=CUTS[1]),
        out_shape=step_shapes(0, CUTS[1]),
        in_specs=[
            pl.BlockSpec(memory_space=pltpu.SMEM),
            pl.BlockSpec(memory_space=pltpu.VMEM),
        ]
        + [pl.BlockSpec(memory_space=pl.ANY)] * 10,
        out_specs=[pl.BlockSpec(memory_space=pltpu.VMEM)] * 2,
        scratch_shapes=[
            pltpu.VMEM((NC, NQ, 2, SIDE, width), BF),
            pltpu.VMEM((2, PW, scale.shape[1]), BF),
            pltpu.VMEM((PW, PW), F32),
            pltpu.VMEM((PW, PW), F32),
            pltpu.VMEM((SIDE, SIDE), F32),
            pltpu.VMEM((SIDE // 8, 64, SIDE), F32),
            pltpu.SemaphoreType.DMA((NC,)),
        ],
        compiler_params=pltpu.CompilerParams(vmem_limit_bytes=VMEM_LIMIT),
        cost_estimate=step_cost(40),
    )(pos, scale, *pieces)


def more_steps(block, first, last):
    return pl.pallas_call(
        functools.partial(inverse_kernel, first=first, last=last),
        out_shape=step_shapes(first, last),
        scratch_shapes=[
            pltpu.VMEM(block.shape, F32),
            pltpu.VMEM((SIDE, SIDE), F32),
            pltpu.VMEM((SIDE // 8, 64, SIDE), F32),
        ],
        compiler_params=pltpu.CompilerParams(vmem_limit_bytes=VMEM_LIMIT),
        cost_estimate=step_cost(1),
    )(block)


def dot3(a, b, dims):
    return dot1(a[0], b[0], dims) + (dot1(a[0], b[1], dims) + dot1(a[1], b[0], dims))


def rows_kernel(pos_ref, scale_ref, rows_hbm, *refs):
    inv_hbm, first, second, refs = refs[:3], refs[3:13], refs[13:23], refs[23:]
    out_ref, buf0, buf1, rbuf, inv, w0, w1, gn, gl, gr, near = refs[:11]
    sem0, sem1, sem2, sem3 = refs[11:]
    count = scale_ref.shape[-1]
    width = buf1.shape[-1]
    own = rbuf.shape[1]
    ones = copies(pos_ref, first, buf0, sem0, count)
    twos = copies(pos_ref, second, buf1, sem1, width)

    def rows_copy(t):
        c = chunk_at(pos_ref, t)
        return pltpu.make_async_copy(rows_hbm.at[c], rbuf.at[c], sem2.at[t])

    def inv_copy(n):
        span = pl.ds(CUTS[n] * SIDE, inv_hbm[n].shape[0])
        return pltpu.make_async_copy(inv_hbm[n], inv.at[span], sem3.at[n])

    def fetch(t):
        for copy in ones[4 * t : 4 * t + 8] + twos[4 * t : 4 * t + 8]:
            copy.start()
        rows_copy(t).start()
        rows_copy(t + 1).start()

    fetch(0)
    for ref in (gn, gl, gr):
        ref[...] = jnp.zeros_like(ref)

    def arrive(t):
        c = chunk_at(pos_ref, t)
        wait_chunk(first[0], buf0, sem0, c, count)
        wait_chunk(second[0], buf1, sem1, c, width)
        rows_copy(t).wait()

    def weighted(t):
        c = chunk_at(pos_ref, t)
        w0[lax.rem(t, 2)] = weigh(scale_ref, c, buf0[c].reshape(PW, count))
        w1[lax.rem(t, 2)] = weigh(scale_ref, c, buf1[c, :, :, :, :count].reshape(PW, count))

    arrive(0)
    fetch(2)
    weighted(0)

    def chunk(t, carry):
        for ahead in range(4, NC, 2):

            @pl.when(t == ahead - 3)
            def _():
                fetch(ahead)

        @pl.when(t == NC - 3)
        def _():
            for n in range(len(inv_hbm)):
                inv_copy(n).start()

        @pl.when(t + 1 < NC)
        def _():
            arrive(t + 1)

        weighted(jnp.minimum(t + 1, NC - 1))
        c = chunk_at(pos_ref, t)
        x1 = buf1[c, :, :, :, :count].reshape(PW, count)
        rows = rbuf[c, :, :count]
        gn[...] += dot1(x1, w0[lax.rem(t, 2)], NT)
        gl[...] += dot1(rows, w0[lax.rem(t, 2)], NT)
        gr[...] += dot1(rows, w1[lax.rem(t, 2)], NT)
        return carry

    lax.fori_loop(0, NC, chunk, 0)

    def source(j):
        start = ((j % 4) * 2 + j // 4) * SIDE
        return slice(start, start + SIDE)

    def put(dst, rows, cols, value):
        dst[0, rows, cols], dst[1, rows, cols] = split2(value)

    def pair(x):
        x = x.astype(F32)
        return x[:, :SIDE] + x[:, SIDE:]

    for j in range(NC):
        cols = slice(j * SIDE, (j + 1) * SIDE)
        put(near, slice(PW, PW + own), cols, gl[:, source(j)] + pair(rbuf[j, :, count:]))
        for i in range(NC):
            prior = buf1[j, i % 4, i // 4, :, count : count + 2 * SIDE]
            put(
                near,
                slice(i * SIDE, (i + 1) * SIDE),
                cols,
                gn[source(i), source(j)] + pair(prior),
            )
    for n in range(len(inv_hbm)):
        inv_copy(n).wait()
    step = 2 * SIDE
    for j in reversed(range(PW // step)):
        k = (j + 1) * step
        cols = slice(j * step, k)
        block = split2(inv[cols, :k])
        for rows in (slice(0, PW), slice(PW, PW + own)):
            put(near, rows, cols, dot3((near[0, rows, :k], near[1, rows, :k]), block, NT))
    for j in range(NC):
        cols = slice(j * SIDE, (j + 1) * SIDE)
        out_ref[j, 0] = near[0, PW:, cols]
        update = dot3(
            (near[0, PW:], near[1, PW:]), (near[0, cols, :], near[1, cols, :]), NT
        )
        out_ref[j, 1] = (gr[:, source(j)] - update).astype(BF)


def own_rows(pos, scale, rows, inverse, first, second):
    count = scale.shape[-1]
    width = first[0].shape[-1]
    own = rows.shape[1]
    return pl.pallas_call(
        rows_kernel,
        out_shape=jax.ShapeDtypeStruct((NC, 2, own, SIDE), BF),
        in_specs=[
            pl.BlockSpec(memory_space=pltpu.SMEM),
            pl.BlockSpec(memory_space=pltpu.VMEM),
        ]
        + [pl.BlockSpec(memory_space=pl.ANY)] * 24,
        out_specs=pl.BlockSpec(memory_space=pltpu.VMEM),
        scratch_shapes=[
            pltpu.VMEM((NC, NQ, 2, SIDE, count), BF),
            pltpu.VMEM((NC, NQ, 2, SIDE, width), BF),
            pltpu.VMEM(rows.shape, BF),
            pltpu.VMEM((PW, PW), F32),
            pltpu.VMEM((2, PW, count), BF),
            pltpu.VMEM((2, PW, count), BF),
            pltpu.VMEM((PW, PW), F32),
            pltpu.VMEM((own, PW), F32),
            pltpu.VMEM((own, PW), F32),
            pltpu.VMEM((2, PW + own, PW), BF),
            pltpu.SemaphoreType.DMA((NC,)),
            pltpu.SemaphoreType.DMA((NC,)),
            pltpu.SemaphoreType.DMA((NC,)),
            pltpu.SemaphoreType.DMA((3,)),
        ],
        compiler_params=pltpu.CompilerParams(vmem_limit_bytes=VMEM_LIMIT),
    )(pos, scale, rows, *inverse, *first, *second)


def body(precision, features, weights_q):
    tcw, ta = precision.shape[0], precision.shape[2]
    count = features.shape[0]
    row, col = lax.axis_index("row"), lax.axis_index("col")
    place = jnp.stack([(row // 2) % 2 * 2 + col % 2, col // 2, row % 2]).astype(jnp.int32)
    tiles = precision.reshape(tcw, ta, SIDE, SIDE)
    hi = lax.reduce_precision(tiles[0, 0], 8, 7)
    lo = tiles[0, 0] - hi
    pack = jnp.concatenate([features[:, 0, 0].T, hi.astype(BF), lo.astype(BF)], axis=1)
    weights = jnp.broadcast_to(weights_q.astype(BF), (NC, 16, count))
    pack, weights = lax.optimization_barrier((pack, weights))
    line = line_of(pack, "x")
    scale = lax.all_to_all(weights, "col", 0, 0, tiled=True)[:, 0].astype(F32) / 64.0
    line = [lax.select_n((x - row // 4) % 4, *line) for x in range(4)]
    packed = pack_rows(features.reshape(count, ta, SIDE), tiles[0])
    near_x, far_x = jnp.stack(line[:2]), jnp.stack(line[2:])
    line = line_of(near_x, "first")
    mine, scale, packed = lax.optimization_barrier((jnp.stack(line), scale, packed))
    nxt, prev = shift(mine, "second", -1), shift(mine, "second", 1)
    first = [mine, nxt, prev] + far_halves(nxt, prev)
    far_x, packed = lax.optimization_barrier((far_x, packed, first[3], first[4]))[:2]
    first += to_other(first)
    rows = lax.all_to_all(packed.reshape(NC, -1, packed.shape[2]), "col", 0, 0, tiled=True)
    far_line = line_of(far_x, "first")
    inv0, block = first_steps(place, scale, first)
    far_line, block, rows = lax.optimization_barrier((far_line, block, rows))
    mine = jnp.stack(far_line)
    nxt, prev = shift(mine, "second", -1), shift(mine, "second", 1)
    inv1, block = more_steps(block, CUTS[1], CUTS[2])
    others = to_other([mine])
    nxt, prev, block = lax.optimization_barrier((nxt, prev, block))
    far = far_halves(nxt, prev)
    others += to_other([nxt, prev])
    inv2 = more_steps(block, CUTS[2], CUTS[3])[0]
    far, inv2 = lax.optimization_barrier((far, inv2))
    second = [mine, nxt, prev] + far + others + to_other(far)
    back = own_rows(place, scale, rows, [inv0, inv1, inv2], first, second)
    back = lax.all_to_all(back, "col", 0, 0, tiled=True).astype(F32)
    back = back.transpose(1, 0, 2, 3).reshape(tcw, ta, SIDE, SIDE)
    row_tile = jnp.arange(ta, dtype=jnp.int32) * lax.axis_size("row") + row
    trailing = jnp.where(row_tile[:, None, None] < PW // SIDE, 0.0, tiles[1] + back[1])
    result = jnp.stack([back[0], trailing])
    return result.reshape(tcw, 1, ta, 1, SIDE, SIDE)


def solution(mesh):
    in_specs = (P(None, "col", None, "row", None, None), P("col", None, "row", None), P("col"))
    out_specs = P(None, "col", None, "row", None, None)
    return jax.shard_map(body, mesh=mesh, in_specs=in_specs, out_specs=out_specs, check_vma=False)
```

```python
import functools

import jax
import jax.numpy as jnp
from jax import lax
from jax.experimental import pallas as pl
from jax.experimental.pallas import tpu as pltpu
from jax.sharding import PartitionSpec as P

PW = 1024
SIDE = 128
NC = 8
NQ = 4
BF = jnp.bfloat16
F32 = jnp.float32
NN = ((1,), (0,))
NT = ((1,), (1,))
TN = ((0,), (0,))
VMEM_LIMIT = 56 << 20


def dot6(a, b, dims=NN):
    return lax.dot_general(
        a, b, (dims, ((), ())), precision=lax.Precision.HIGHEST, preferred_element_type=F32
    )


def dot1(a, b, dims=NN):
    return lax.dot_general(a, b, (dims, ((), ())), preferred_element_type=F32)


def split2(x):
    hi = x.astype(BF)
    return hi, (x - hi.astype(F32)).astype(BF)


def flat(x, y, z, core):
    return ((x * 2 + y // 2) * 2 + core) * NC + z * 2 + y % 2


def shift_pairs(kind, by):
    out = []
    for x in range(4):
        for y in range(4):
            for z in range(4):
                for core in range(2):
                    nx, ny, nz, nc = x, y, z, core
                    if kind == "x":
                        nx = (x + by) % 4
                    elif kind == "core":
                        nc = 1 - core
                    elif (kind == "first") == (core == 0):
                        ny = (y + by) % 4
                    else:
                        nz = (z + by) % 4
                    out.append((flat(x, y, z, core), flat(nx, ny, nz, nc)))
    return out


def shift(x, kind, by=1):
    return lax.ppermute(x, ("row", "col"), shift_pairs(kind, by))


def line_of(u, kind):
    return [u, shift(u, kind, -1), shift(u, kind, 2), shift(u, kind, 1)]


def far_halves(nxt, prev):
    half = nxt.shape[0] // 2
    return [shift(prev[:half], "second", 1), shift(nxt[half:], "second", -1)]


def to_other(pieces):
    return [shift(p, "core") for p in pieces]


def piece_at(first, second):
    if second == 2:
        return (3, first) if first < 2 else (4, first - 2)
    return ((0, 1, None, 2)[second], first)


def chip_of(pos_ref, i, j):
    core = pos_ref[2]
    y = lax.rem(pos_ref[0] + jnp.where(core == 0, i, j), 4)
    z = lax.rem(pos_ref[1] + jnp.where(core == 0, j, i), 4)
    return y, z


def copies(pos_ref, pieces, buf, sems, width):
    out = []
    for i0, j0 in ((0, 0), (0, 1), (1, 0), (1, 1)):
        for i, j in ((i0, j0), (i0 + 2, j0), (i0, j0 + 2), (i0 + 2, j0 + 2)):
            y, z = chip_of(pos_ref, i, j)
            c = z * 2 + lax.rem(y, 2)
            for other in range(2):
                core = 1 - pos_ref[2] if other else pos_ref[2]
                n, k = piece_at(j, i) if other else piece_at(i, j)
                out.append(
                    pltpu.make_async_copy(
                        pieces[5 * other + n].at[k, :, :, pl.ds(0, width)],
                        buf.at[c, lax.div(y, 2) * 2 + core],
                        sems.at[c],
                    )
                )
    return out


def chunk_at(pos_ref, t):
    i, j = lax.div(t, 4), lax.rem(lax.div(t, 2), 2)
    y, z = chip_of(pos_ref, i, j)
    return lax.rem(z + 2 * lax.rem(t, 2), 4) * 2 + lax.rem(y, 2)


def wait_chunk(piece_ref, buf, sems, c, width):
    for q in range(NQ):
        pltpu.make_async_copy(
            piece_ref.at[0, :, :, pl.ds(0, width)], buf.at[c, q], sems.at[c]
        ).wait()


def pack_kernel(features_ref, prior_ref, out_ref):
    count = features_ref.shape[0]
    for a in range(features_ref.shape[1]):
        out_ref[a, :, :count] = features_ref[:, a, :].T
        hi, lo = split2(prior_ref[a])
        out_ref[a, :, count : count + SIDE] = hi
        out_ref[a, :, count + SIDE :] = lo


def pack_rows(features, prior):
    count, ta, _ = features.shape
    return pl.pallas_call(
        pack_kernel,
        out_shape=jax.ShapeDtypeStruct((ta, SIDE, count + 2 * SIDE), BF),
        compiler_params=pltpu.CompilerParams(vmem_limit_bytes=VMEM_LIMIT),
    )(features, prior)


def weigh(scale_ref, c, x):
    return (scale_ref[pl.ds(c, 1), :] * x.astype(F32)).astype(BF)


def top_block(pos_ref, scale_ref, pieces, buf, wbuf, g_ref, a, sems):
    width = buf.shape[-1]
    count = scale_ref.shape[-1]
    for copy in copies(pos_ref, pieces, buf, sems, width):
        copy.start()
    g_ref[...] = jnp.zeros_like(g_ref)

    def weighted(t):
        c = chunk_at(pos_ref, t)
        x = buf[c, :, :, :, :count].reshape(PW, count)
        wbuf[lax.rem(t, 2)] = weigh(scale_ref, c, x)

    wait_chunk(pieces[0], buf, sems, chunk_at(pos_ref, 0), width)
    weighted(0)

    def chunk(t, carry):
        @pl.when(t + 1 < NC)
        def _():
            wait_chunk(pieces[0], buf, sems, chunk_at(pos_ref, t + 1), width)

        weighted(jnp.minimum(t + 1, NC - 1))
        x = buf[chunk_at(pos_ref, t), :, :, :, :count].reshape(PW, count)
        g_ref[...] += dot1(x, wbuf[lax.rem(t, 2)], NT)
        return carry

    lax.fori_loop(0, NC, chunk, 0)

    def tile(i, j):
        ri, rj = ((i % 4) * 2 + i // 4) * SIDE, ((j % 4) * 2 + j // 4) * SIDE
        return g_ref[ri : ri + SIDE, rj : rj + SIDE]

    for i in range(NC):
        for j in range(i, NC):
            prior = buf[j, i % 4, i // 4, :, count : count + 2 * SIDE].astype(F32)
            a[i * SIDE : (i + 1) * SIDE, j * SIDE : (j + 1) * SIDE] = 0.5 * (
                tile(i, j) + tile(j, i).T
            ) + (prior[:, :SIDE] + prior[:, SIDE:])


def factor(groups, spread):
    m = list(groups)
    full = m[0].shape
    lane = lax.broadcasted_iota(jnp.int32, full, 1)
    sub = lax.broadcasted_iota(jnp.int32, full, 0)
    done = []
    for p in range(len(m)):
        base = 8 * p
        inside = (lane >= base) & (lane < base + 8)
        e = [jnp.broadcast_to(m[p][:, base + j : base + j + 1], full) for j in range(8)]
        for j in range(8):
            spread[p, 8 * j : 8 * j + 8, :] = e[j]
        s = {
            (l, j): jnp.broadcast_to(spread[p, 8 * j + l : 8 * j + l + 1, :], full)
            for j in range(8)
            for l in range(j, 8)
        }
        own = jnp.where(inside, jnp.where(lane - base == sub, 1.0, 0.0), m[p])
        w = [jnp.broadcast_to(own[l : l + 1, :], full) for l in range(8)]
        t = {}
        v = [None] * 8
        for j in range(8):
            d = s[j, j]
            r = 1.0 / d
            v[j] = w[j] * lax.rsqrt(d)
            w[j] = w[j] * r
            for l in range(j + 1, 8):
                t[j, l] = s[l, j] * r
            for l in range(8):
                if l == j:
                    continue
                w[l] = w[l] - (s[l, j] if l > j else t[l, j]) * w[j]
                if l > j:
                    for k in range(j + 1, l + 1):
                        s[l, k] = s[l, k] - s[l, j] * t[j, k]
                else:
                    for k in range(j + 1, 8):
                        t[l, k] = t[l, k] - t[l, j] * t[j, k]
        for g in range(p + 1, len(m)):
            c = [jnp.broadcast_to(m[g][:, base + j : base + j + 1], full) * w[j] for j in range(8)]
            total = ((c[0] + c[1]) + (c[2] + c[3])) + ((c[4] + c[5]) + (c[6] + c[7]))
            m[g] = jnp.where(inside, 0.0, m[g]) - total
        rows = v[0]
        for j in range(1, 8):
            rows = jnp.where(sub == j, v[j], rows)
        done.append(jnp.where(lane <= sub + base, rows, 0.0))
    return done


def inverse_kernel(a_in, *refs, first, last):
    refs[-3][...] = a_in[...]
    block_steps(refs[:-3], *refs[-3:], first, last)


def top_kernel(pos_ref, scale_ref, *refs, last):
    pieces, outs, (buf, wbuf, g_ref, a, m_ref, spread, sems) = refs[:10], refs[10:-7], refs[-7:]
    top_block(pos_ref, scale_ref, pieces, buf, wbuf, g_ref, a, sems)
    block_steps(outs, a, m_ref, spread, 0, last)


def block_steps(outs, a, m_ref, spread, first, last):
    inv_ref = outs[0]
    order = a.shape[1]
    nb = order // SIDE

    def rows(i):
        return slice((i - first) * SIDE, (i - first + 1) * SIDE)

    def cols(i, j):
        return slice(i * SIDE, j * SIDE)

    def below(k, i, v):
        vi = v[:, cols(i, i + 1)]
        left = dot6(vi, v[:, : (k + 1) * SIDE], TN)
        if k:
            a[rows(i), cols(0, k)] = a[rows(i), cols(0, k)] - left[:, : k * SIDE]
        a[rows(i), cols(k, k + 1)] = -left[:, k * SIDE :]
        start = i if i > k + 1 else i + 1
        if start < nb:
            a[rows(i), cols(start, nb)] = a[rows(i), cols(start, nb)] - dot6(
                vi, v[:, start * SIDE :], TN
            )

    later = []
    for k in range(first, last):
        here, own = rows(k), cols(k, k + 1)
        groups = [
            a[here.start + 8 * g : here.start + 8 * g + 8, own] for g in range(SIDE // 8)
        ]
        for g, group in enumerate(factor(groups, spread)):
            m_ref[8 * g : 8 * g + 8, :] = group
        for k0, i, v in later:
            below(k0, i, v)
        later = []
        linv = m_ref[...]
        parts = [dot6(linv, a[here, cols(0, k)])] if k else []
        parts.append(linv)
        if k + 1 < nb:
            side = dot6(linv, a[here, cols(k + 1, k + 2)])
            diag = cols(k + 1, k + 2)
            a[rows(k + 1), diag] = a[rows(k + 1), diag] - dot6(side, side, TN)
            parts.append(side)
        if k + 2 < nb:
            parts.append(dot6(linv, a[here, cols(k + 2, nb)]))
        v = jnp.concatenate(parts, axis=1)
        inv_ref[here, : (k + 1) * SIDE] = v[:, : (k + 1) * SIDE]
        if k + 1 < nb:
            inv_ref[here, (k + 1) * SIDE :] = jnp.zeros((SIDE, order - (k + 1) * SIDE), F32)
        later = [(k, i, v) for i in range(k + 1, nb)]
    for k0, i, v in later:
        below(k0, i, v)
    if last < nb:
        outs[1][...] = a[(last - first) * SIDE :, :]


CUTS = (0, 3, 6, 8)


def step_shapes(first, last):
    shapes = [jax.ShapeDtypeStruct(((last - first) * SIDE, PW), F32)]
    if last < NC:
        shapes.append(jax.ShapeDtypeStruct((PW - last * SIDE, PW), F32))
    return shapes


def step_cost(us):
    return pl.CostEstimate(flops=us * 10**9, bytes_accessed=10**6, transcendentals=0)


def first_steps(pos, scale, pieces):
    width = pieces[0].shape[-1]
    return pl.pallas_call(
        functools.partial(top_kernel, last=CUTS[1]),
        out_shape=step_shapes(0, CUTS[1]),
        in_specs=[
            pl.BlockSpec(memory_space=pltpu.SMEM),
            pl.BlockSpec(memory_space=pltpu.VMEM),
        ]
        + [pl.BlockSpec(memory_space=pl.ANY)] * 10,
        out_specs=[pl.BlockSpec(memory_space=pltpu.VMEM)] * 2,
        scratch_shapes=[
            pltpu.VMEM((NC, NQ, 2, SIDE, width), BF),
            pltpu.VMEM((2, PW, scale.shape[1]), BF),
            pltpu.VMEM((PW, PW), F32),
            pltpu.VMEM((PW, PW), F32),
            pltpu.VMEM((SIDE, SIDE), F32),
            pltpu.VMEM((SIDE // 8, 64, SIDE), F32),
            pltpu.SemaphoreType.DMA((NC,)),
        ],
        compiler_params=pltpu.CompilerParams(vmem_limit_bytes=VMEM_LIMIT),
        cost_estimate=step_cost(40),
    )(pos, scale, *pieces)


def more_steps(block, first, last):
    return pl.pallas_call(
        functools.partial(inverse_kernel, first=first, last=last),
        out_shape=step_shapes(first, last),
        scratch_shapes=[
            pltpu.VMEM(block.shape, F32),
            pltpu.VMEM((SIDE, SIDE), F32),
            pltpu.VMEM((SIDE // 8, 64, SIDE), F32),
        ],
        compiler_params=pltpu.CompilerParams(vmem_limit_bytes=VMEM_LIMIT),
        cost_estimate=step_cost(1),
    )(block)


def dot3(a, b, dims):
    return dot1(a[0], b[0], dims) + (dot1(a[0], b[1], dims) + dot1(a[1], b[0], dims))


def rows_kernel(pos_ref, scale_ref, rows_hbm, *refs):
    inv_hbm, first, second, refs = refs[:3], refs[3:13], refs[13:23], refs[23:]
    out_ref, buf0, buf1, rbuf, inv, w0, w1, gn, gl, gr, near = refs[:11]
    sem0, sem1, sem2, sem3 = refs[11:]
    count = scale_ref.shape[-1]
    width = buf1.shape[-1]
    own = rbuf.shape[1]
    ones = copies(pos_ref, first, buf0, sem0, count)
    twos = copies(pos_ref, second, buf1, sem1, width)

    def rows_copy(t):
        c = chunk_at(pos_ref, t)
        return pltpu.make_async_copy(rows_hbm.at[c], rbuf.at[c], sem2.at[t])

    def inv_copy(n):
        span = pl.ds(CUTS[n] * SIDE, inv_hbm[n].shape[0])
        return pltpu.make_async_copy(inv_hbm[n], inv.at[span], sem3.at[n])

    def fetch(t):
        for copy in ones[4 * t : 4 * t + 8] + twos[4 * t : 4 * t + 8]:
            copy.start()
        rows_copy(t).start()
        rows_copy(t + 1).start()

    fetch(0)
    for ref in (gn, gl, gr):
        ref[...] = jnp.zeros_like(ref)

    def arrive(t):
        c = chunk_at(pos_ref, t)
        wait_chunk(first[0], buf0, sem0, c, count)
        wait_chunk(second[0], buf1, sem1, c, width)
        rows_copy(t).wait()

    def weighted(t):
        c = chunk_at(pos_ref, t)
        w0[lax.rem(t, 2)] = weigh(scale_ref, c, buf0[c].reshape(PW, count))
        w1[lax.rem(t, 2)] = weigh(scale_ref, c, buf1[c, :, :, :, :count].reshape(PW, count))

    arrive(0)
    fetch(2)
    weighted(0)

    def chunk(t, carry):
        for ahead in range(4, NC, 2):

            @pl.when(t == ahead - 3)
            def _():
                fetch(ahead)

        @pl.when(t == NC - 3)
        def _():
            for n in range(len(inv_hbm)):
                inv_copy(n).start()

        @pl.when(t + 1 < NC)
        def _():
            arrive(t + 1)

        weighted(jnp.minimum(t + 1, NC - 1))
        c = chunk_at(pos_ref, t)
        x1 = buf1[c, :, :, :, :count].reshape(PW, count)
        rows = rbuf[c, :, :count]
        gn[...] += dot1(x1, w0[lax.rem(t, 2)], NT)
        gl[...] += dot1(rows, w0[lax.rem(t, 2)], NT)
        gr[...] += dot1(rows, w1[lax.rem(t, 2)], NT)
        return carry

    lax.fori_loop(0, NC, chunk, 0)

    def source(j):
        start = ((j % 4) * 2 + j // 4) * SIDE
        return slice(start, start + SIDE)

    def put(dst, rows, cols, value):
        dst[0, rows, cols], dst[1, rows, cols] = split2(value)

    def pair(x):
        x = x.astype(F32)
        return x[:, :SIDE] + x[:, SIDE:]

    for j in range(NC):
        cols = slice(j * SIDE, (j + 1) * SIDE)
        put(near, slice(PW, PW + own), cols, gl[:, source(j)] + pair(rbuf[j, :, count:]))
        for i in range(NC):
            prior = buf1[j, i % 4, i // 4, :, count : count + 2 * SIDE]
            put(
                near,
                slice(i * SIDE, (i + 1) * SIDE),
                cols,
                gn[source(i), source(j)] + pair(prior),
            )
    for n in range(len(inv_hbm)):
        inv_copy(n).wait()
    step = 2 * SIDE
    for j in reversed(range(PW // step)):
        k = (j + 1) * step
        cols = slice(j * step, k)
        block = split2(inv[cols, :k])
        for rows in (slice(0, PW), slice(PW, PW + own)):
            put(near, rows, cols, dot3((near[0, rows, :k], near[1, rows, :k]), block, NT))
    for j in range(0, NC, 2):
        cols = slice(j * SIDE, (j + 2) * SIDE)
        update = dot3((near[0, PW:], near[1, PW:]), (near[0, cols, :], near[1, cols, :]), NT)
        for i in range(2):
            part = slice(i * SIDE, (i + 1) * SIDE)
            out_ref[j + i, 0] = near[0, PW:, (j + i) * SIDE : (j + i + 1) * SIDE]
            out_ref[j + i, 1] = (gr[:, source(j + i)] - update[:, part]).astype(BF)


def own_rows(pos, scale, rows, inverse, first, second):
    count = scale.shape[-1]
    width = first[0].shape[-1]
    own = rows.shape[1]
    return pl.pallas_call(
        rows_kernel,
        out_shape=jax.ShapeDtypeStruct((NC, 2, own, SIDE), BF),
        in_specs=[
            pl.BlockSpec(memory_space=pltpu.SMEM),
            pl.BlockSpec(memory_space=pltpu.VMEM),
        ]
        + [pl.BlockSpec(memory_space=pl.ANY)] * 24,
        out_specs=pl.BlockSpec(memory_space=pltpu.VMEM),
        scratch_shapes=[
            pltpu.VMEM((NC, NQ, 2, SIDE, count), BF),
            pltpu.VMEM((NC, NQ, 2, SIDE, width), BF),
            pltpu.VMEM(rows.shape, BF),
            pltpu.VMEM((PW, PW), F32),
            pltpu.VMEM((2, PW, count), BF),
            pltpu.VMEM((2, PW, count), BF),
            pltpu.VMEM((PW, PW), F32),
            pltpu.VMEM((own, PW), F32),
            pltpu.VMEM((own, PW), F32),
            pltpu.VMEM((2, PW + own, PW), BF),
            pltpu.SemaphoreType.DMA((NC,)),
            pltpu.SemaphoreType.DMA((NC,)),
            pltpu.SemaphoreType.DMA((NC,)),
            pltpu.SemaphoreType.DMA((3,)),
        ],
        compiler_params=pltpu.CompilerParams(vmem_limit_bytes=VMEM_LIMIT),
    )(pos, scale, rows, *inverse, *first, *second)


def body(precision, features, weights_q):
    tcw, ta = precision.shape[0], precision.shape[2]
    count = features.shape[0]
    row, col = lax.axis_index("row"), lax.axis_index("col")
    place = jnp.stack([(row // 2) % 2 * 2 + col % 2, col // 2, row % 2]).astype(jnp.int32)
    tiles = precision.reshape(tcw, ta, SIDE, SIDE)
    hi = lax.reduce_precision(tiles[0, 0], 8, 7)
    lo = tiles[0, 0] - hi
    pack = jnp.concatenate([features[:, 0, 0].T, hi.astype(BF), lo.astype(BF)], axis=1)
    weights = jnp.broadcast_to(weights_q.astype(BF), (NC, 16, count))
    pack, weights = lax.optimization_barrier((pack, weights))
    line = line_of(pack, "x")
    scale = lax.all_to_all(weights, "col", 0, 0, tiled=True)[:, 0].astype(F32) / 64.0
    line = [lax.select_n((x - row // 4) % 4, *line) for x in range(4)]
    packed = pack_rows(features.reshape(count, ta, SIDE), tiles[0])
    near_x, far_x = jnp.stack(line[:2]), jnp.stack(line[2:])
    line = line_of(near_x, "first")
    mine, scale, packed = lax.optimization_barrier((jnp.stack(line), scale, packed))
    nxt, prev = shift(mine, "second", -1), shift(mine, "second", 1)
    first = [mine, nxt, prev] + far_halves(nxt, prev)
    far_x, packed = lax.optimization_barrier((far_x, packed, first[3], first[4]))[:2]
    first += to_other(first)
    rows = lax.all_to_all(packed.reshape(NC, -1, packed.shape[2]), "col", 0, 0, tiled=True)
    far_line = line_of(far_x, "first")
    inv0, block = first_steps(place, scale, first)
    far_line, block, rows = lax.optimization_barrier((far_line, block, rows))
    mine = jnp.stack(far_line)
    nxt, prev = shift(mine, "second", -1), shift(mine, "second", 1)
    inv1, block = more_steps(block, CUTS[1], CUTS[2])
    others = to_other([mine])
    nxt, prev, block = lax.optimization_barrier((nxt, prev, block))
    far = far_halves(nxt, prev)
    others += to_other([nxt, prev])
    inv2 = more_steps(block, CUTS[2], CUTS[3])[0]
    far, inv2 = lax.optimization_barrier((far, inv2))
    second = [mine, nxt, prev] + far + others + to_other(far)
    back = own_rows(place, scale, rows, [inv0, inv1, inv2], first, second)
    back = lax.all_to_all(back, "col", 0, 0, tiled=True).astype(F32)
    back = back.transpose(1, 0, 2, 3).reshape(tcw, ta, SIDE, SIDE)
    row_tile = jnp.arange(ta, dtype=jnp.int32) * lax.axis_size("row") + row
    trailing = jnp.where(row_tile[:, None, None] < PW // SIDE, 0.0, tiles[1] + back[1])
    result = jnp.stack([back[0], trailing])
    return result.reshape(tcw, 1, ta, 1, SIDE, SIDE)


def solution(mesh):
    in_specs = (P(None, "col", None, "row", None, None), P("col", None, "row", None), P("col"))
    out_specs = P(None, "col", None, "row", None, None)
    return jax.shard_map(body, mesh=mesh, in_specs=in_specs, out_specs=out_specs, check_vma=False)
```

```python
import functools

import jax
import jax.numpy as jnp
from jax import lax
from jax.experimental import pallas as pl
from jax.experimental.pallas import tpu as pltpu
from jax.sharding import PartitionSpec as P

PW = 1024
SIDE = 128
NC = 8
NQ = 4
BF = jnp.bfloat16
F32 = jnp.float32
NN = ((1,), (0,))
NT = ((1,), (1,))
TN = ((0,), (0,))
VMEM_LIMIT = 56 << 20


def dot6(a, b, dims=NN):
    return lax.dot_general(
        a, b, (dims, ((), ())), precision=lax.Precision.HIGHEST, preferred_element_type=F32
    )


def dot1(a, b, dims=NN):
    return lax.dot_general(a, b, (dims, ((), ())), preferred_element_type=F32)


def split2(x):
    hi = x.astype(BF)
    return hi, (x - hi.astype(F32)).astype(BF)


def flat(x, y, z, core):
    return ((x * 2 + y // 2) * 2 + core) * NC + z * 2 + y % 2


def shift_pairs(kind, by):
    out = []
    for x in range(4):
        for y in range(4):
            for z in range(4):
                for core in range(2):
                    nx, ny, nz, nc = x, y, z, core
                    if kind == "x":
                        nx = (x + by) % 4
                    elif kind == "core":
                        nc = 1 - core
                    elif (kind == "first") == (core == 0):
                        ny = (y + by) % 4
                    else:
                        nz = (z + by) % 4
                    out.append((flat(x, y, z, core), flat(nx, ny, nz, nc)))
    return out


def shift(x, kind, by=1):
    return lax.ppermute(x, ("row", "col"), shift_pairs(kind, by))


def line_of(u, kind):
    return [u, shift(u, kind, -1), shift(u, kind, 2), shift(u, kind, 1)]


def far_halves(nxt, prev):
    half = nxt.shape[0] // 2
    return [shift(prev[:half], "second", 1), shift(nxt[half:], "second", -1)]


def to_other(pieces):
    return [shift(p, "core") for p in pieces]


def piece_at(first, second):
    if second == 2:
        return (3, first) if first < 2 else (4, first - 2)
    return ((0, 1, None, 2)[second], first)


def chip_of(pos_ref, i, j):
    core = pos_ref[2]
    y = lax.rem(pos_ref[0] + jnp.where(core == 0, i, j), 4)
    z = lax.rem(pos_ref[1] + jnp.where(core == 0, j, i), 4)
    return y, z


def copies(pos_ref, pieces, buf, sems, width):
    out = []
    for i0, j0 in ((0, 0), (0, 1), (1, 0), (1, 1)):
        for i, j in ((i0, j0), (i0 + 2, j0), (i0, j0 + 2), (i0 + 2, j0 + 2)):
            y, z = chip_of(pos_ref, i, j)
            c = z * 2 + lax.rem(y, 2)
            for other in range(2):
                core = 1 - pos_ref[2] if other else pos_ref[2]
                n, k = piece_at(j, i) if other else piece_at(i, j)
                out.append(
                    pltpu.make_async_copy(
                        pieces[5 * other + n].at[k, :, :, pl.ds(0, width)],
                        buf.at[c, lax.div(y, 2) * 2 + core],
                        sems.at[c],
                    )
                )
    return out


def chunk_at(pos_ref, t):
    i, j = lax.div(t, 4), lax.rem(lax.div(t, 2), 2)
    y, z = chip_of(pos_ref, i, j)
    return lax.rem(z + 2 * lax.rem(t, 2), 4) * 2 + lax.rem(y, 2)


def wait_chunk(piece_ref, buf, sems, c, width):
    for q in range(NQ):
        pltpu.make_async_copy(
            piece_ref.at[0, :, :, pl.ds(0, width)], buf.at[c, q], sems.at[c]
        ).wait()


def pack_kernel(features_ref, prior_ref, out_ref):
    count = features_ref.shape[0]
    for a in range(features_ref.shape[1]):
        out_ref[a, :, :count] = features_ref[:, a, :].T
        hi, lo = split2(prior_ref[a])
        out_ref[a, :, count : count + SIDE] = hi
        out_ref[a, :, count + SIDE :] = lo


def pack_rows(features, prior):
    count, ta, _ = features.shape
    return pl.pallas_call(
        pack_kernel,
        out_shape=jax.ShapeDtypeStruct((ta, SIDE, count + 2 * SIDE), BF),
        compiler_params=pltpu.CompilerParams(vmem_limit_bytes=VMEM_LIMIT),
    )(features, prior)


def weigh(scale_ref, c, x):
    return (scale_ref[pl.ds(c, 1), :] * x.astype(F32)).astype(BF)


def top_block(pos_ref, scale_ref, pieces, buf, wbuf, g_ref, a, sems):
    width = buf.shape[-1]
    count = scale_ref.shape[-1]
    for copy in copies(pos_ref, pieces, buf, sems, width):
        copy.start()
    g_ref[...] = jnp.zeros_like(g_ref)

    def weighted(t):
        c = chunk_at(pos_ref, t)
        x = buf[c, :, :, :, :count].reshape(PW, count)
        wbuf[lax.rem(t, 2)] = weigh(scale_ref, c, x)

    wait_chunk(pieces[0], buf, sems, chunk_at(pos_ref, 0), width)
    weighted(0)

    def chunk(t, carry):
        @pl.when(t + 1 < NC)
        def _():
            wait_chunk(pieces[0], buf, sems, chunk_at(pos_ref, t + 1), width)

        weighted(jnp.minimum(t + 1, NC - 1))
        x = buf[chunk_at(pos_ref, t), :, :, :, :count].reshape(PW, count)
        g_ref[...] += dot1(x, wbuf[lax.rem(t, 2)], NT)
        return carry

    lax.fori_loop(0, NC, chunk, 0)

    def tile(i, j):
        ri, rj = ((i % 4) * 2 + i // 4) * SIDE, ((j % 4) * 2 + j // 4) * SIDE
        return g_ref[ri : ri + SIDE, rj : rj + SIDE]

    for i in range(NC):
        for j in range(i, NC):
            prior = buf[j, i % 4, i // 4, :, count : count + 2 * SIDE].astype(F32)
            a[i * SIDE : (i + 1) * SIDE, j * SIDE : (j + 1) * SIDE] = 0.5 * (
                tile(i, j) + tile(j, i).T
            ) + (prior[:, :SIDE] + prior[:, SIDE:])


def factor(groups, spread):
    m = list(groups)
    full = m[0].shape
    lane = lax.broadcasted_iota(jnp.int32, full, 1)
    sub = lax.broadcasted_iota(jnp.int32, full, 0)
    done = []
    for p in range(len(m)):
        base = 8 * p
        inside = (lane >= base) & (lane < base + 8)
        e = [jnp.broadcast_to(m[p][:, base + j : base + j + 1], full) for j in range(8)]
        if spread is not None:
            for j in range(8):
                spread[p, 8 * j : 8 * j + 8, :] = e[j]
        s = {}
        for j in range(8):
            for l in range(j, 8):
                one = e[j][l : l + 1, :]
                if spread is not None:
                    one = spread[p, 8 * j + l : 8 * j + l + 1, :]
                s[l, j] = jnp.broadcast_to(one, full)
        own = jnp.where(inside, jnp.where(lane - base == sub, 1.0, 0.0), m[p])
        w = [jnp.broadcast_to(own[l : l + 1, :], full) for l in range(8)]
        t = {}
        v = [None] * 8
        for j in range(8):
            d = s[j, j]
            r = 1.0 / d
            v[j] = w[j] * lax.rsqrt(d)
            w[j] = w[j] * r
            for l in range(j + 1, 8):
                t[j, l] = s[l, j] * r
            for l in range(8):
                if l == j:
                    continue
                w[l] = w[l] - (s[l, j] if l > j else t[l, j]) * w[j]
                if l > j:
                    for k in range(j + 1, l + 1):
                        s[l, k] = s[l, k] - s[l, j] * t[j, k]
                else:
                    for k in range(j + 1, 8):
                        t[l, k] = t[l, k] - t[l, j] * t[j, k]
        for g in range(p + 1, len(m)):
            c = [jnp.broadcast_to(m[g][:, base + j : base + j + 1], full) * w[j] for j in range(8)]
            total = ((c[0] + c[1]) + (c[2] + c[3])) + ((c[4] + c[5]) + (c[6] + c[7]))
            m[g] = jnp.where(inside, 0.0, m[g]) - total
        rows = v[0]
        for j in range(1, 8):
            rows = jnp.where(sub == j, v[j], rows)
        done.append(jnp.where(lane <= sub + base, rows, 0.0))
    return done


def inverse_kernel(a_in, *refs, first, last):
    refs[-3][...] = a_in[...]
    block_steps(refs[:-3], *refs[-3:], first, last)


def top_kernel(pos_ref, scale_ref, *refs, last):
    pieces, outs, (buf, wbuf, g_ref, a, m_ref, sems) = refs[:10], refs[10:-6], refs[-6:]
    top_block(pos_ref, scale_ref, pieces, buf, wbuf, g_ref, a, sems)
    block_steps(outs, a, m_ref, None, 0, last)


def block_steps(outs, a, m_ref, spread, first, last):
    inv_ref = outs[0]
    order = a.shape[1]
    nb = order // SIDE

    def rows(i):
        return slice((i - first) * SIDE, (i - first + 1) * SIDE)

    def cols(i, j):
        return slice(i * SIDE, j * SIDE)

    def below(k, i, v):
        vi = v[:, cols(i, i + 1)]
        left = dot6(vi, v[:, : (k + 1) * SIDE], TN)
        if k:
            a[rows(i), cols(0, k)] = a[rows(i), cols(0, k)] - left[:, : k * SIDE]
        a[rows(i), cols(k, k + 1)] = -left[:, k * SIDE :]
        start = i if i > k + 1 else i + 1
        if start < nb:
            a[rows(i), cols(start, nb)] = a[rows(i), cols(start, nb)] - dot6(
                vi, v[:, start * SIDE :], TN
            )

    later = []
    for k in range(first, last):
        here, own = rows(k), cols(k, k + 1)
        groups = [
            a[here.start + 8 * g : here.start + 8 * g + 8, own] for g in range(SIDE // 8)
        ]
        for g, group in enumerate(factor(groups, spread)):
            m_ref[8 * g : 8 * g + 8, :] = group
        for k0, i, v in later:
            below(k0, i, v)
        later = []
        linv = m_ref[...]
        parts = [dot6(linv, a[here, cols(0, k)])] if k else []
        parts.append(linv)
        if k + 1 < nb:
            side = dot6(linv, a[here, cols(k + 1, k + 2)])
            diag = cols(k + 1, k + 2)
            a[rows(k + 1), diag] = a[rows(k + 1), diag] - dot6(side, side, TN)
            parts.append(side)
        if k + 2 < nb:
            parts.append(dot6(linv, a[here, cols(k + 2, nb)]))
        v = jnp.concatenate(parts, axis=1)
        inv_ref[here, : (k + 1) * SIDE] = v[:, : (k + 1) * SIDE]
        if k + 1 < nb:
            inv_ref[here, (k + 1) * SIDE :] = jnp.zeros((SIDE, order - (k + 1) * SIDE), F32)
        later = [(k, i, v) for i in range(k + 1, nb)]
    for k0, i, v in later:
        below(k0, i, v)
    if last < nb:
        outs[1][...] = a[(last - first) * SIDE :, :]


CUTS = (0, 3, 6, 8)


def step_shapes(first, last):
    shapes = [jax.ShapeDtypeStruct(((last - first) * SIDE, PW), F32)]
    if last < NC:
        shapes.append(jax.ShapeDtypeStruct((PW - last * SIDE, PW), F32))
    return shapes


def step_cost(us):
    return pl.CostEstimate(flops=us * 10**9, bytes_accessed=10**6, transcendentals=0)


def first_steps(pos, scale, pieces):
    width = pieces[0].shape[-1]
    return pl.pallas_call(
        functools.partial(top_kernel, last=CUTS[1]),
        out_shape=step_shapes(0, CUTS[1]),
        in_specs=[
            pl.BlockSpec(memory_space=pltpu.SMEM),
            pl.BlockSpec(memory_space=pltpu.VMEM),
        ]
        + [pl.BlockSpec(memory_space=pl.ANY)] * 10,
        out_specs=[pl.BlockSpec(memory_space=pltpu.VMEM)] * 2,
        scratch_shapes=[
            pltpu.VMEM((NC, NQ, 2, SIDE, width), BF),
            pltpu.VMEM((2, PW, scale.shape[1]), BF),
            pltpu.VMEM((PW, PW), F32),
            pltpu.VMEM((PW, PW), F32),
            pltpu.VMEM((SIDE, SIDE), F32),
            pltpu.SemaphoreType.DMA((NC,)),
        ],
        compiler_params=pltpu.CompilerParams(vmem_limit_bytes=VMEM_LIMIT),
        cost_estimate=step_cost(40),
    )(pos, scale, *pieces)


def more_steps(block, first, last):
    return pl.pallas_call(
        functools.partial(inverse_kernel, first=first, last=last),
        out_shape=step_shapes(first, last),
        scratch_shapes=[
            pltpu.VMEM(block.shape, F32),
            pltpu.VMEM((SIDE, SIDE), F32),
            pltpu.VMEM((SIDE // 8, 64, SIDE), F32),
        ],
        compiler_params=pltpu.CompilerParams(vmem_limit_bytes=VMEM_LIMIT),
        cost_estimate=step_cost(1),
    )(block)


def dot3(a, b, dims):
    return dot1(a[0], b[0], dims) + (dot1(a[0], b[1], dims) + dot1(a[1], b[0], dims))


def rows_kernel(pos_ref, scale_ref, rows_hbm, *refs):
    inv_hbm, first, second, refs = refs[:3], refs[3:13], refs[13:23], refs[23:]
    out_ref, buf0, buf1, rbuf, inv, w0, w1, gn, gl, gr, near = refs[:11]
    sem0, sem1, sem2, sem3 = refs[11:]
    count = scale_ref.shape[-1]
    width = buf1.shape[-1]
    own = rbuf.shape[1]
    ones = copies(pos_ref, first, buf0, sem0, count)
    twos = copies(pos_ref, second, buf1, sem1, width)

    def rows_copy(t):
        c = chunk_at(pos_ref, t)
        return pltpu.make_async_copy(rows_hbm.at[c], rbuf.at[c], sem2.at[t])

    def inv_copy(n):
        span = pl.ds(CUTS[n] * SIDE, inv_hbm[n].shape[0])
        return pltpu.make_async_copy(inv_hbm[n], inv.at[span], sem3.at[n])

    def fetch(t):
        for copy in ones[4 * t : 4 * t + 8] + twos[4 * t : 4 * t + 8]:
            copy.start()
        rows_copy(t).start()
        rows_copy(t + 1).start()

    fetch(0)
    for ref in (gn, gl, gr):
        ref[...] = jnp.zeros_like(ref)

    def arrive(t):
        c = chunk_at(pos_ref, t)
        wait_chunk(first[0], buf0, sem0, c, count)
        wait_chunk(second[0], buf1, sem1, c, width)
        rows_copy(t).wait()

    def weighted(t):
        c = chunk_at(pos_ref, t)
        w0[lax.rem(t, 2)] = weigh(scale_ref, c, buf0[c].reshape(PW, count))
        w1[lax.rem(t, 2)] = weigh(scale_ref, c, buf1[c, :, :, :, :count].reshape(PW, count))

    arrive(0)
    fetch(2)
    weighted(0)

    def chunk(t, carry):
        for ahead in range(4, NC, 2):

            @pl.when(t == ahead - 3)
            def _():
                fetch(ahead)

        @pl.when(t == NC - 3)
        def _():
            for n in range(len(inv_hbm)):
                inv_copy(n).start()

        @pl.when(t + 1 < NC)
        def _():
            arrive(t + 1)

        weighted(jnp.minimum(t + 1, NC - 1))
        c = chunk_at(pos_ref, t)
        x1 = buf1[c, :, :, :, :count].reshape(PW, count)
        rows = rbuf[c, :, :count]
        gn[...] += dot1(x1, w0[lax.rem(t, 2)], NT)
        gl[...] += dot1(rows, w0[lax.rem(t, 2)], NT)
        gr[...] += dot1(rows, w1[lax.rem(t, 2)], NT)
        return carry

    lax.fori_loop(0, NC, chunk, 0)

    def source(j):
        start = ((j % 4) * 2 + j // 4) * SIDE
        return slice(start, start + SIDE)

    def put(dst, rows, cols, value):
        dst[0, rows, cols], dst[1, rows, cols] = split2(value)

    def pair(x):
        x = x.astype(F32)
        return x[:, :SIDE] + x[:, SIDE:]

    for j in range(NC):
        cols = slice(j * SIDE, (j + 1) * SIDE)
        put(near, slice(PW, PW + own), cols, gl[:, source(j)] + pair(rbuf[j, :, count:]))
        for i in range(NC):
            prior = buf1[j, i % 4, i // 4, :, count : count + 2 * SIDE]
            put(
                near,
                slice(i * SIDE, (i + 1) * SIDE),
                cols,
                gn[source(i), source(j)] + pair(prior),
            )
    for n in range(len(inv_hbm)):
        inv_copy(n).wait()
    step = 2 * SIDE
    for j in reversed(range(PW // step)):
        k = (j + 1) * step
        cols = slice(j * step, k)
        block = split2(inv[cols, :k])
        for rows in (slice(0, PW), slice(PW, PW + own)):
            put(near, rows, cols, dot3((near[0, rows, :k], near[1, rows, :k]), block, NT))
    for j in range(0, NC, 2):
        cols = slice(j * SIDE, (j + 2) * SIDE)
        update = dot3((near[0, PW:], near[1, PW:]), (near[0, cols, :], near[1, cols, :]), NT)
        for i in range(2):
            part = slice(i * SIDE, (i + 1) * SIDE)
            out_ref[j + i, 0] = near[0, PW:, (j + i) * SIDE : (j + i + 1) * SIDE]
            out_ref[j + i, 1] = (gr[:, source(j + i)] - update[:, part]).astype(BF)


def own_rows(pos, scale, rows, inverse, first, second):
    count = scale.shape[-1]
    width = first[0].shape[-1]
    own = rows.shape[1]
    return pl.pallas_call(
        rows_kernel,
        out_shape=jax.ShapeDtypeStruct((NC, 2, own, SIDE), BF),
        in_specs=[
            pl.BlockSpec(memory_space=pltpu.SMEM),
            pl.BlockSpec(memory_space=pltpu.VMEM),
        ]
        + [pl.BlockSpec(memory_space=pl.ANY)] * 24,
        out_specs=pl.BlockSpec(memory_space=pltpu.VMEM),
        scratch_shapes=[
            pltpu.VMEM((NC, NQ, 2, SIDE, count), BF),
            pltpu.VMEM((NC, NQ, 2, SIDE, width), BF),
            pltpu.VMEM(rows.shape, BF),
            pltpu.VMEM((PW, PW), F32),
            pltpu.VMEM((2, PW, count), BF),
            pltpu.VMEM((2, PW, count), BF),
            pltpu.VMEM((PW, PW), F32),
            pltpu.VMEM((own, PW), F32),
            pltpu.VMEM((own, PW), F32),
            pltpu.VMEM((2, PW + own, PW), BF),
            pltpu.SemaphoreType.DMA((NC,)),
            pltpu.SemaphoreType.DMA((NC,)),
            pltpu.SemaphoreType.DMA((NC,)),
            pltpu.SemaphoreType.DMA((3,)),
        ],
        compiler_params=pltpu.CompilerParams(vmem_limit_bytes=VMEM_LIMIT),
    )(pos, scale, rows, *inverse, *first, *second)


def body(precision, features, weights_q):
    tcw, ta = precision.shape[0], precision.shape[2]
    count = features.shape[0]
    row, col = lax.axis_index("row"), lax.axis_index("col")
    place = jnp.stack([(row // 2) % 2 * 2 + col % 2, col // 2, row % 2]).astype(jnp.int32)
    tiles = precision.reshape(tcw, ta, SIDE, SIDE)
    hi = lax.reduce_precision(tiles[0, 0], 8, 7)
    lo = tiles[0, 0] - hi
    pack = jnp.concatenate([features[:, 0, 0].T, hi.astype(BF), lo.astype(BF)], axis=1)
    weights = jnp.broadcast_to(weights_q.astype(BF), (NC, 16, count))
    pack, weights = lax.optimization_barrier((pack, weights))
    line = line_of(pack, "x")
    scale = lax.all_to_all(weights, "col", 0, 0, tiled=True)[:, 0].astype(F32) / 64.0
    line = [lax.select_n((x - row // 4) % 4, *line) for x in range(4)]
    packed = pack_rows(features.reshape(count, ta, SIDE), tiles[0])
    near_x, far_x = jnp.stack(line[:2]), jnp.stack(line[2:])
    line = line_of(near_x, "first")
    mine, scale, packed = lax.optimization_barrier((jnp.stack(line), scale, packed))
    nxt, prev = shift(mine, "second", -1), shift(mine, "second", 1)
    first = [mine, nxt, prev] + far_halves(nxt, prev)
    far_x, packed = lax.optimization_barrier((far_x, packed, first[3], first[4]))[:2]
    first += to_other(first)
    rows = lax.all_to_all(packed.reshape(NC, -1, packed.shape[2]), "col", 0, 0, tiled=True)
    far_line = line_of(far_x, "first")
    inv0, block = first_steps(place, scale, first)
    far_line, block, rows = lax.optimization_barrier((far_line, block, rows))
    mine = jnp.stack(far_line)
    nxt, prev = shift(mine, "second", -1), shift(mine, "second", 1)
    inv1, block = more_steps(block, CUTS[1], CUTS[2])
    others = to_other([mine])
    nxt, prev, block = lax.optimization_barrier((nxt, prev, block))
    far = far_halves(nxt, prev)
    others += to_other([nxt, prev])
    inv2 = more_steps(block, CUTS[2], CUTS[3])[0]
    far, inv2 = lax.optimization_barrier((far, inv2))
    second = [mine, nxt, prev] + far + others + to_other(far)
    back = own_rows(place, scale, rows, [inv0, inv1, inv2], first, second)
    back = lax.all_to_all(back, "col", 0, 0, tiled=True).astype(F32)
    back = back.transpose(1, 0, 2, 3).reshape(tcw, ta, SIDE, SIDE)
    row_tile = jnp.arange(ta, dtype=jnp.int32) * lax.axis_size("row") + row
    trailing = jnp.where(row_tile[:, None, None] < PW // SIDE, 0.0, tiles[1] + back[1])
    result = jnp.stack([back[0], trailing])
    return result.reshape(tcw, 1, ta, 1, SIDE, SIDE)


def solution(mesh):
    in_specs = (P(None, "col", None, "row", None, None), P("col", None, "row", None), P("col"))
    out_specs = P(None, "col", None, "row", None, None)
    return jax.shard_map(body, mesh=mesh, in_specs=in_specs, out_specs=out_specs, check_vma=False)
```
